32 devices in a mesh: group: 2 (over y), blk: 8 (over z, x), split: 2 (over core).
Axes of the slice: x: 2, y: 2, z: 4, core: 2. Of those that a mesh axis runs over, the one named last changes fastest.
Arguments:
- embeddings: bfloat16 [128, 256, 768], P(('group', 'blk', 'split')), parts along dimension 0
- lengths: int32 [128], P(('group', 'blk', 'split')), parts along dimension 0, may hold values from 16 to 256, as said below
Outputs:
- pair_f1: float32 [128, 2, 2, 8], P(('group', 'blk', 'split')), parts along dimension 0
- utility: float32 [128], P(('group', 'blk', 'split')), parts along dimension 0
The draws below stay inside these ranges and needn't reach their ends.
There are 2 independent parts, one for each index of `group`. The reference program is written for one: setup_inputs(seed, part) draws one part's arguments, and reference() takes and returns one part's arrays. A program takes and returns all parts, laid end to end along the dimension named above; each array names one. Nothing has to cross between parts.
Inputs may be any that keep to these rules, and one draw needn't show every extreme that they name: `lengths`: lengths lie between 16 and 256; some candidate has exactly 256 tokens and some exactly 16.
All inputs are finite; a program needn't handle non-finite values.
Results may differ from the reference program's by a relative error of at most 0.0003.
Values may be sent and summed in bfloat16 or wider, within the bound.
No kernel may reach another device: no remote copies, remote signals or barrier semaphores. Data moves between devices by JAX's collectives and lax.ppermute only.
A program may use at most 64 MiB of HBM per device.

```python
import math
import jax
import jax.numpy as jnp
from jax import lax

WIDTH = 768
TOK = 256
ROUNDS = 2
BLOCK = 8
CANDS = 64
N_BLK = 8


def draw_embeddings(key, part):
    key = jax.random.fold_in(key, 11)
    key_snippet, key_pick, key_start, key_share, key_source, key_random = jax.random.split(key, 6)
    key_vocab, key_noise, key_spread = jax.random.split(jax.random.fold_in(key, 5), 3)
    vocab_count = max(64, 8 * TOK)
    snippet_count = 4
    snippets = jax.random.randint(key_snippet, (snippet_count, 2 * TOK), 0, vocab_count)
    snippet_pick = jax.random.randint(key_pick, (CANDS,), 0, snippet_count)
    start_at = jax.random.randint(key_start, (CANDS,), 0, TOK + 1)
    share_level = jax.random.randint(key_share, (CANDS, 1), 2, 10)
    from_snippet = jax.random.randint(key_source, (CANDS, TOK), 0, 10) < share_level
    random_ids = jax.random.randint(key_random, (CANDS, TOK), 0, vocab_count)
    positions = start_at[:, None] + jnp.arange(TOK)[None, :]
    snippet_ids = snippets[snippet_pick[:, None], positions]
    token_ids = jnp.where(from_snippet, snippet_ids, random_ids)
    vocabulary = jax.random.normal(key_vocab, (vocab_count, WIDTH), jnp.float32)
    context_noise = jax.random.normal(key_noise, (CANDS, TOK, WIDTH), jnp.float32)
    spread = jnp.exp(jax.random.uniform(key_spread, (CANDS, TOK, 1), jnp.float32, 0.0, math.log(10.0)))
    tokens_float = vocabulary[token_ids] + 0.3 * context_noise
    return (spread * tokens_float).astype(jnp.bfloat16)


def draw_lengths(key, part):
    key = jax.random.fold_in(key, 23)
    key_first, key_second, key_place, key_offset = jax.random.split(key, 4)
    shortest = max(1, TOK // 16)
    first_draw = jax.random.randint(key_first, (CANDS,), shortest, TOK + 1)
    second_draw = jax.random.randint(key_second, (CANDS,), shortest, TOK + 1)
    counts = jnp.minimum(first_draw, second_draw)
    longest_at = jax.random.randint(key_place, (), 0, CANDS)
    shortest_at = (longest_at + 1 + jax.random.randint(key_offset, (), 0, CANDS - 1)) % CANDS
    counts = counts.at[longest_at].set(TOK).at[shortest_at].set(shortest)
    return counts.astype(jnp.int32)


def setup_inputs(seed: int = 0, part: int = 0) -> dict:
    key_list = jax.random.split(jax.random.key(seed), 3)
    part_keys = jax.random.split(jax.random.fold_in(key_list[2], part), 3)
    return {
        "embeddings": draw_embeddings(jax.random.fold_in(jax.random.fold_in(key_list[2], part), 71), part),
        "lengths": draw_lengths(jax.random.fold_in(jax.random.fold_in(key_list[2], part), 71), part),
    }


def normalize(embeds):
    values = embeds.astype(jnp.float32)
    inverse = lax.rsqrt(lax.optimization_barrier(jnp.mean(values * values, axis=-1, keepdims=True)) + 1e-06)
    return (values * inverse * values.shape[-1] ** (-0.5)).astype(jnp.bfloat16)

def pair_scores(own_unit, own_lengths, partner, partner_lengths):
    members, tokens, features = partner.shape
    flattened = partner.reshape(members * tokens, features)
    partner_mask = jnp.arange(tokens)[None, :] < partner_lengths[:, None]
    partner_float = partner_lengths.astype(jnp.float32)

    def score_one(element):
        own_row, own_length = element
        similar = lax.dot_general(own_row, flattened, (((1,), (1,)), ((), ())), preferred_element_type=jnp.float32)
        similar = similar.reshape(tokens, members, tokens)
        row_mask = jnp.arange(tokens) < own_length
        best_row = lax.optimization_barrier(jnp.max(jnp.where(partner_mask[None], similar, jnp.float32(-3.0)), axis=2))
        precision = lax.optimization_barrier(jnp.sum(jnp.where(row_mask[:, None], best_row, jnp.float32(0.0)), axis=0)) / own_length.astype(jnp.float32)
        best_col = lax.optimization_barrier(jnp.max(jnp.where(row_mask[:, None, None], similar, jnp.float32(-3.0)), axis=0))
        recall = lax.optimization_barrier(jnp.sum(jnp.where(partner_mask, best_col, jnp.float32(0.0)), axis=1)) / partner_float
        return 2.0 * precision * recall / jnp.maximum(precision + recall, 0.5)
    return lax.map(score_one, (own_unit, own_lengths))

def reference(embeddings, lengths):
    unit_emb = normalize(embeddings).reshape(N_BLK, BLOCK, TOK, WIDTH)
    block_lengths = lengths.reshape(N_BLK, BLOCK)
    tile_list = []
    for round_index in range(ROUNDS):
        distance = round_index + 1
        partner_emb = jnp.roll(unit_emb, -distance, axis=0)
        partner_len = jnp.roll(block_lengths, -distance, axis=0)

        def block_scores(element):
            return pair_scores(element[0], element[1], element[2], element[3])
        forward = lax.map(block_scores, (unit_emb, block_lengths, partner_emb, partner_len))
        backward = jnp.swapaxes(jnp.roll(forward, distance, axis=0), 1, 2)
        tile_list.append(jnp.stack([forward, backward], axis=2))
    pair_f1 = jnp.stack(tile_list, axis=2).reshape(CANDS, ROUNDS, 2, BLOCK)
    utility = lax.optimization_barrier(jnp.mean(pair_f1, axis=(1, 2, 3)))
    return (pair_f1, utility)
```

```python
import functools
import jax
import jax.numpy as jnp
from jax import lax
from jax.experimental import pallas as pl
from jax.experimental.pallas import tpu as pltpu
from jax.sharding import PartitionSpec as P

GRAIN = 16
ROWS = 128
LANES = 128
VMEM_LIMIT = 48 * 1024 * 1024


def z_route(blocks):
    hop = lambda b: (b - 2) % blocks if b % 2 == 0 else (b + 2) % blocks
    return [(b * 2 + s, hop(b) * 2 + s) for b in range(blocks) for s in range(2)]


def x_route(blocks):
    hop = lambda b, s: (b + 1, 1 - s) if b % 2 == 0 else (b - 1, s)
    return [(b * 2 + s, hop(b, s)[0] * 2 + hop(b, s)[1]) for b in range(blocks) for s in range(2)]


def back(route):
    return [(target, source) for source, target in route]


def grains(length):
    return (length + (GRAIN - 1)) // GRAIN


def pack_kernel(lengths_ref, embeds_ref, out_ref):
    candidate = pl.program_id(0)
    tokens, width = embeds_ref.shape[1:]
    start = jnp.int32(0)
    for i in range(lengths_ref.shape[0] - 1):
        start += jnp.where(i < candidate, grains(lengths_ref[i]) * GRAIN, 0)
    values = embeds_ref[0].astype(jnp.float32)
    inverse = lax.rsqrt(jnp.mean(values * values, axis=-1, keepdims=True) + 1e-06)
    unit = values * inverse * width ** (-0.5)
    inside = lax.broadcasted_iota(jnp.int32, (tokens, 1), 0) < lengths_ref[candidate]
    unit = jnp.where(inside, unit, unit[0:1])
    out_ref[pl.ds(pl.multiple_of(start, GRAIN), tokens), :] = unit.astype(out_ref.dtype)


def pack(embeddings, lengths):
    members, tokens, width = embeddings.shape
    return pl.pallas_call(
        pack_kernel,
        grid=(members,),
        out_shape=jax.ShapeDtypeStruct((members * tokens, width), embeddings.dtype),
        in_specs=[
            pl.BlockSpec(memory_space=pltpu.SMEM),
            pl.BlockSpec((1, tokens, width), lambda i: (i, 0, 0)),
        ],
        out_specs=pl.BlockSpec((members * tokens, width), lambda i: (0, 0)),
        compiler_params=pltpu.CompilerParams(vmem_limit_bytes=VMEM_LIMIT),
        name="pack",
    )(lengths, embeddings)


def score_kernel(
    every_ref, place_ref, own_hbm, twin_hbm, side_hbm, far_hbm, out_ref,
    own, twin, side, far, side_wide, far_wide, cols, rows, sems,
):
    members = every_ref.shape[1]
    tokens = far_wide.shape[0] // members
    copies = [
        pltpu.make_async_copy(source, target, sems.at[k])
        for k, (source, target) in enumerate(
            ((far_hbm, far), (own_hbm, own), (side_hbm, side), (twin_hbm, twin))
        )
    ]
    for copy in copies:
        copy.start()

    def lengths_of(k):
        return [every_ref[place_ref[k], i] for i in range(members)]

    own_len, twin_len, side_len, far_len = [lengths_of(k) for k in range(4)]

    def starts_of(lengths):
        starts = [jnp.int32(0)]
        for length in lengths:
            starts.append(starts[-1] + grains(length))
        return starts

    def widen(packed, lengths, wide):
        starts = starts_of(lengths)
        for j in range(members):
            for g in range(tokens // GRAIN):
                here = jnp.where(g * GRAIN < lengths[j], starts[j] + g, starts[j])
                source = pl.ds(pl.multiple_of(here * GRAIN, GRAIN), GRAIN)
                wide[pl.ds(j * tokens + g * GRAIN, GRAIN), :] = packed[source, :]

    lane = lax.broadcasted_iota(jnp.int32, (1, LANES), 1)
    token = lax.broadcasted_iota(jnp.int32, (1, tokens), 1)
    row = lax.broadcasted_iota(jnp.int32, (tokens, 1), 0)

    def job(left, left_len, wide, wide_len, place):
        starts = starts_of(left_len)
        blocks = (starts[-1] * GRAIN + (ROWS - 1)) // ROWS

        def step(k, carry):
            part = left[pl.ds(pl.multiple_of(k * ROWS, ROWS), ROWS), :]
            best = jnp.zeros((ROWS, LANES), jnp.float32)
            for j in range(members):
                similar = lax.dot_general(
                    part,
                    wide[j * tokens : (j + 1) * tokens, :],
                    (((1,), (1,)), ((), ())),
                    preferred_element_type=jnp.float32,
                )
                best = jnp.where(lane == j, jnp.max(similar, axis=1, keepdims=True), best)
                folded = similar.reshape(ROWS // GRAIN, 2, GRAIN // 2, tokens)
                folded = jnp.max(folded, axis=1).reshape(ROWS // 2, tokens)
                cols[
                    pl.ds(pl.multiple_of(k * (ROWS // 2), ROWS // 2), ROWS // 2),
                    j * tokens : (j + 1) * tokens,
                ] = folded
            rows[pl.ds(pl.multiple_of(k * ROWS, ROWS), ROWS), :] = best
            return carry

        lax.fori_loop(0, blocks, step, 0)
        for i in range(members):
            first = pl.multiple_of(starts[i] * GRAIN, GRAIN)
            window = rows[pl.ds(first, tokens), :]
            total = jnp.sum(jnp.where(row < left_len[i], window, 0.0), axis=0, keepdims=True)
            precision = total / left_len[i].astype(jnp.float32)

            def widest(g, best, i=i):
                here = pl.multiple_of((starts[i] + g) * (GRAIN // 2), GRAIN // 2)
                return jnp.maximum(best, cols[pl.ds(here, GRAIN // 2), :])

            best = lax.fori_loop(
                0,
                grains(left_len[i]),
                widest,
                jnp.full((GRAIN // 2, members * tokens), -3.0, jnp.float32),
            )
            best = jnp.max(best, axis=0, keepdims=True)
            recall = jnp.zeros((1, LANES), jnp.float32)
            for j in range(members):
                piece = best[:, j * tokens : (j + 1) * tokens]
                total = jnp.sum(
                    jnp.where(token < wide_len[j], piece, 0.0), axis=1, keepdims=True
                )
                recall = jnp.where(lane == j, total / wide_len[j].astype(jnp.float32), recall)
            score = 2.0 * precision * recall / jnp.maximum(precision + recall, 0.5)
            out_ref[place + i : place + i + 1, :] = jnp.where(lane < members, score, 0.0)

    copies[0].wait()
    widen(far, far_len, far_wide)
    copies[1].wait()
    job(own, own_len, far_wide, far_len, 0)
    copies[2].wait()
    job(side, side_len, far_wide, far_len, 2 * members)
    widen(side, side_len, side_wide)
    job(own, own_len, side_wide, side_len, 3 * members)
    copies[3].wait()
    job(twin, twin_len, far_wide, far_len, members)


def score(every, place, own, twin, side, far):
    members = every.shape[1]
    count, width = own.shape
    spare = count + count // members
    whole = pltpu.VMEM((count, width), own.dtype)
    return pl.pallas_call(
        score_kernel,
        out_shape=jax.ShapeDtypeStruct((4 * members, LANES), jnp.float32),
        in_specs=[pl.BlockSpec(memory_space=pltpu.SMEM)] * 2
        + [pl.BlockSpec(memory_space=pl.ANY)] * 4,
        out_specs=pl.BlockSpec(memory_space=pltpu.VMEM),
        scratch_shapes=[whole] * 6
        + [
            pltpu.VMEM((count // 2, count), jnp.float32),
            pltpu.VMEM((spare, LANES), jnp.float32),
            pltpu.SemaphoreType.DMA((4,)),
        ],
        compiler_params=pltpu.CompilerParams(vmem_limit_bytes=VMEM_LIMIT),
        name="score",
    )(every, place, own, twin, side, far)


def assemble_kernel(place_ref, own_ref, twin_ref, side_ref, far_ref, pairs_ref, mean_ref):
    members = pairs_ref.shape[0]
    odd = place_ref[4] == 1
    second = place_ref[5] == 1
    held = own_ref.shape[0]
    both = jnp.concatenate(
        [side_ref[...], far_ref[...], jnp.zeros((LANES - 2 * held, LANES), jnp.float32)], axis=0
    )
    turned = both.T
    lane = lax.broadcasted_iota(jnp.int32, (members, LANES), 1)

    def straight(ref, k):
        return ref[k * members : (k + 1) * members, :]

    def across(which, k):
        first = which * held + k * members
        return pltpu.roll(turned, (LANES - first) % LANES, 1)[:members, :]

    one, four = straight(own_ref, 3), straight(side_ref, 2)
    two, three = across(0, 3), across(1, 2)
    five, six = straight(own_ref, 0), straight(twin_ref, 1)
    seven, eight = across(1, 0), across(1, 1)

    def join(same, other):
        low = jnp.where(second, other, same)
        high = pltpu.roll(jnp.where(second, same, other), members, 1)
        return jnp.where(lane < members, low, jnp.where(lane < 2 * members, high, 0.0))

    pick = lambda a, b: jnp.where(odd, b, a)
    parts = [
        [
            join(pick(one, four), pick(two, three)),
            join(pick(three, two), pick(four, one)),
        ],
        [
            join(pick(five, seven), pick(six, eight)),
            join(pick(seven, five), pick(eight, six)),
        ],
    ]
    total = jnp.zeros((members, LANES), jnp.float32)
    for r in range(2):
        for d in range(2):
            total = total + parts[r][d]
            for i in range(members):
                pairs_ref[i, r, d : d + 1, :] = parts[r][d][i : i + 1, : 2 * members]
    mean = jnp.sum(total, axis=1, keepdims=True) / (8.0 * members)
    diagonal = lane == lax.broadcasted_iota(jnp.int32, (members, LANES), 0)
    mean_ref[...] = jnp.sum(jnp.where(diagonal, mean, 0.0), axis=0, keepdims=True)[:, :members]


def assemble(place, own, twin, side, far, members):
    return pl.pallas_call(
        assemble_kernel,
        out_shape=(
            jax.ShapeDtypeStruct((members, 2, 2, 2 * members), jnp.float32),
            jax.ShapeDtypeStruct((1, members), jnp.float32),
        ),
        in_specs=[pl.BlockSpec(memory_space=pltpu.SMEM)]
        + [pl.BlockSpec(memory_space=pltpu.VMEM)] * 4,
        out_specs=[pl.BlockSpec(memory_space=pltpu.VMEM)] * 2,
        name="assemble",
    )(place, own, twin, side, far)


def on_device(embeddings, lengths):
    members = lengths.shape[0]
    blocks, cores = lax.axis_size("blk"), lax.axis_size("split")
    axes = ("blk", "split")
    far_path, side_path = z_route(blocks), x_route(blocks)
    twin_path = [(0, 1), (1, 0)]

    block, core = lax.axis_index("blk"), lax.axis_index("split")
    parity = block % 2
    far_block = (block + 2 - 4 * parity) % blocks
    side_block = block + 1 - 2 * parity
    side_core = jnp.where(parity == 1, 1 - core, core)
    place = jnp.stack(
        [
            block * cores + core,
            block * cores + 1 - core,
            side_block * cores + side_core,
            far_block * cores + core,
            parity,
            core,
        ]
    ).astype(jnp.int32)

    packed = pack(embeddings, lengths)
    far = lax.ppermute(packed, axes, far_path)
    side = lax.ppermute(packed, axes, side_path)
    twin = lax.ppermute(packed, "split", twin_path)
    told = jnp.broadcast_to(lengths[None, :], (blocks * cores, members))
    every = lax.all_to_all(told, axes, 0, 0, tiled=True)

    scores = score(every, place, packed, twin, side, far)
    far_scores = lax.ppermute(scores, axes, back(far_path))
    side_scores = lax.ppermute(scores, axes, back(side_path))
    twin_scores = lax.ppermute(scores, "split", twin_path)
    pair_f1, utility = assemble(place, scores, twin_scores, side_scores, far_scores, members)
    return (pair_f1, utility.reshape(members))


def solution(mesh):
    placed = (P(("group", "blk", "split"), None, None), P(("group", "blk", "split")))
    return jax.shard_map(
        on_device,
        mesh=mesh,
        in_specs=placed,
        out_specs=(P(("group", "blk", "split"), None, None, None), P(("group", "blk", "split"))),
        check_vma=False,
    )
```

```python
import functools
import jax
import jax.numpy as jnp
from jax import lax
from jax.experimental import pallas as pl
from jax.experimental.pallas import tpu as pltpu
from jax.sharding import PartitionSpec as P

GRAIN = 16
TILE = 256
UNROLL = 4
LANES = 128
HEAD = GRAIN
VMEM_LIMIT = 56 * 1024 * 1024
SCORE_VMEM = 28 * 1024 * 1024


def z_route(blocks):
    hop = lambda b: (b - 2) % blocks if b % 2 == 0 else (b + 2) % blocks
    return [(b * 2 + s, hop(b) * 2 + s) for b in range(blocks) for s in range(2)]


def x_route(blocks):
    hop = lambda b, s: (b + 1, 1 - s) if b % 2 == 0 else (b - 1, s)
    return [(b * 2 + s, hop(b, s)[0] * 2 + hop(b, s)[1]) for b in range(blocks) for s in range(2)]


def back(route):
    return [(target, source) for source, target in route]


def grains(length):
    return (length + (GRAIN - 1)) // GRAIN


def starts_of(lengths):
    starts = [jnp.int32(HEAD // GRAIN)]
    for length in lengths:
        starts.append(starts[-1] + grains(length))
    return starts


def pack_kernel(lengths_hbm, embeds_hbm, packed_hbm, one_hbm, two_hbm, lengths, embeds, packed, sems):
    members, tokens, width = embeds_hbm.shape
    told = pltpu.make_async_copy(lengths_hbm, lengths, sems.at[members])
    told.start()
    loads = [
        pltpu.make_async_copy(embeds_hbm.at[i], embeds.at[i], sems.at[i]) for i in range(members)
    ]
    for load in loads:
        load.start()
    told.wait()
    row = lax.broadcasted_iota(jnp.int32, (HEAD, width), 0)
    head = jnp.zeros((HEAD, width), jnp.float32)
    for i in range(members):
        head = jnp.where(row == i, lengths[i].astype(jnp.float32), head)
    packed[0:HEAD, :] = head.astype(packed.dtype)
    starts = starts_of([lengths[i] for i in range(members)])
    token = lax.broadcasted_iota(jnp.int32, (tokens, 1), 0)
    for i in range(members):
        loads[i].wait()
        values = embeds[i].astype(jnp.float32)
        inverse = lax.rsqrt(jnp.mean(values * values, axis=-1, keepdims=True) + 1e-06)
        unit = values * inverse * width ** (-0.5)
        unit = jnp.where(token < lengths[i], unit, unit[0:1])
        first = pl.multiple_of(starts[i] * GRAIN, GRAIN)
        packed[pl.ds(first, tokens), :] = unit.astype(packed.dtype)
    one, two = one_hbm.shape[0], two_hbm.shape[0]
    stores = [
        pltpu.make_async_copy(packed.at[0:one], one_hbm, sems.at[0]),
        pltpu.make_async_copy(packed.at[one : one + two], two_hbm, sems.at[1]),
        pltpu.make_async_copy(packed, packed_hbm, sems.at[2]),
    ]
    for store in stores:
        store.start()
    for store in stores:
        store.wait()


def pack(embeddings, lengths, one, two):
    members, tokens, width = embeddings.shape
    count = HEAD + members * tokens
    array = lambda rows: jax.ShapeDtypeStruct((rows, width), embeddings.dtype)
    return pl.pallas_call(
        pack_kernel,
        out_shape=(array(count), array(one), array(two)),
        in_specs=[pl.BlockSpec(memory_space=pl.ANY)] * 2,
        out_specs=[pl.BlockSpec(memory_space=pl.ANY)] * 3,
        scratch_shapes=[
            pltpu.SMEM((members,), jnp.int32),
            pltpu.VMEM((members, tokens, width), embeddings.dtype),
            pltpu.VMEM((count, width), embeddings.dtype),
            pltpu.SemaphoreType.DMA((members + 1,)),
        ],
        compiler_params=pltpu.CompilerParams(vmem_limit_bytes=VMEM_LIMIT),
        name="pack",
    )(lengths, embeddings)


def score_kernel(pieces, before, members, has_past, *refs):
    own, twin = refs[:2]
    sides, fars = refs[2 : 2 + pieces], refs[2 + pieces : 2 + 2 * pieces]
    refs = refs[2 + 2 * pieces :]
    past_ref = refs[0] if has_past else None
    out_ref, needs_ref, side, wide, cols, rows, totals, peaks, sems = refs[int(has_past) :]
    count = own.shape[0]
    tokens = (count - HEAD) // members
    now = sum(piece.shape[0] for piece in fars)

    copies, at = [], 0
    for k, piece in enumerate(sides):
        size = piece.shape[0]
        copies.append(pltpu.make_async_copy(piece, side.at[at : at + size], sems.at[k]))
        at += size
    for copy in copies:
        copy.start()

    def lengths_of(ref):
        head = ref[0:HEAD, 0:LANES].astype(jnp.float32)
        return [jnp.max(head[i : i + 1, :]).astype(jnp.int32) for i in range(members)]

    lens = [lengths_of(ref) for ref in (own, twin, sides[0])]
    starts = [starts_of(each) for each in lens]
    side_len, far_len = lens[2], lengths_of(fars[0])
    side_start, far_start = starts[2], starts_of(far_len)
    for k, start in enumerate((starts[0], side_start, far_start)):
        needs_ref[k] = start[-1] * GRAIN

    def state(start):
        ends = [start[i + 1] * GRAIN for i in range(members)]
        return [end <= now for end in ends], [end <= before for end in ends]

    side_now, side_old = state(side_start)
    far_now, far_old = state(far_start)
    side_new = [jnp.logical_and(a, jnp.logical_not(b)) for a, b in zip(side_now, side_old)]
    far_new = [jnp.logical_and(a, jnp.logical_not(b)) for a, b in zip(far_now, far_old)]

    def tiles(start):
        return ((start[-1] - HEAD // GRAIN) * GRAIN + (TILE - 1)) // TILE

    own_tiles, twin_tiles = tiles(starts[0]), tiles(starts[1])
    side_end = jnp.int32(HEAD // GRAIN)
    side_from = jnp.int32(HEAD // GRAIN)
    for i in range(members):
        side_end = jnp.where(side_now[i], side_start[i + 1], side_end)
        side_from = jnp.where(side_old[i], side_start[i + 1], side_from)
    side_tiles = ((side_end - HEAD // GRAIN) * GRAIN + (TILE - 1)) // TILE
    side_first = jnp.where(
        side_end > side_from, (side_from - HEAD // GRAIN) * GRAIN // TILE, side_tiles
    )
    slots = 2 * members
    zero = jnp.int32(0)

    def pick(refs, first):
        at, found = 0, None
        for ref in refs:
            size = ref.shape[0]
            here = jnp.clip(first - at, 0, size - GRAIN)
            rows = ref[pl.ds(pl.multiple_of(here, GRAIN), GRAIN), :]
            found = rows if found is None else jnp.where(first >= at, rows, found)
            at += size
        return found

    used = []
    for j in range(members):
        used.append(jnp.logical_and(far_now[j], jnp.logical_or(far_new[j], side_end > side_from)))
    used += side_new
    for k in range(slots):
        source, start, lengths = (
            (fars, far_start, far_len) if k < members else (sides, side_start, side_len)
        )
        j = k % members

        @pl.when(used[k])
        def _(k=k, j=j, source=source, start=start, lengths=lengths):
            for g in range(tokens // GRAIN):
                here = jnp.where(g * GRAIN < lengths[j], start[j] + g, start[j])
                wide[k, g * GRAIN : (g + 1) * GRAIN, :] = pick(source, here * GRAIN)

    lane = lax.broadcasted_iota(jnp.int32, (1, LANES), 1)

    def sweep(left, base, begins, ends):
        sums = [zero]
        for begin, end in zip(begins, ends):
            sums.append(sums[-1] + end - begin)
        total = sums[-1]

        def place_of(t):
            t = jnp.minimum(t, total - 1)
            slot, local = zero, t + begins[0]
            for k in range(1, len(begins)):
                slot = jnp.where(t >= sums[k], k, slot)
                local = jnp.where(t >= sums[k], t - sums[k] + begins[k], local)
            return slot, HEAD + local * TILE

        def step(n, carry):
            places = [place_of(n * UNROLL + u) for u in range(UNROLL)]
            found = []
            for slot, first in places:
                part = left[pl.ds(pl.multiple_of(first, GRAIN), TILE), :]
                found.append(
                    lax.dot_general(
                        part,
                        wide[slot],
                        (((1,), (1,)), ((), ())),
                        preferred_element_type=jnp.float32,
                    )
                )
            for (slot, first), similar in zip(places, found):
                folded = similar.reshape(TILE // GRAIN, 2, GRAIN // 2, tokens)
                folded = jnp.max(folded, axis=1).reshape(TILE // 2, tokens)
                here = pl.ds(pl.multiple_of((base + first) // 2, GRAIN // 2), TILE // 2)
                cols[slot, here, :] = folded
                best = jnp.max(similar, axis=1, keepdims=True)
                here = pl.ds(pl.multiple_of(base + first, GRAIN), TILE)
                rows[here, :] = jnp.where(lane == slot, best, rows[here, :])
            return carry

        lax.fori_loop(0, (total + (UNROLL - 1)) // UNROLL, step, 0)

    far_own = [jnp.where(new, own_tiles, 0) for new in far_new]
    side_own = [jnp.where(new, own_tiles, 0) for new in side_new]
    sweep(own, 0, [zero] * slots, far_own + side_own)
    sweep(twin, count, [zero] * members, [jnp.where(new, twin_tiles, 0) for new in far_new])
    for copy in copies:
        copy.wait()
    begins = [jnp.where(new, 0, side_first) for new in far_new]
    ends = [jnp.where(here, side_tiles, begin) for here, begin in zip(far_now, begins)]
    sweep(side, 2 * count, begins, ends)

    token = lax.broadcasted_iota(jnp.int32, (1, tokens), 1)
    row = lax.broadcasted_iota(jnp.int32, (tokens, 1), 0)
    any_used = used[0]
    for flag in used[1:]:
        any_used = jnp.logical_or(any_used, flag)

    @pl.when(any_used)
    def _():
        for which in range(3):
            width = slots if which == 0 else members
            for i in range(members):
                length = lens[which][i]
                seat = which * members + i
                first = which * count + starts[which][i] * GRAIN
                window = rows[pl.ds(pl.multiple_of(first, GRAIN), tokens), :]
                window = jnp.sum(jnp.where(row < length, window, 0.0), axis=0, keepdims=True)
                totals[seat : seat + 1, :] = window / length.astype(jnp.float32)
                last = grains(length) - 1

                def widest(n, best, first=first, last=last, width=width):
                    best = list(best)
                    for u in range(4):
                        here = first // 2 + jnp.minimum(n * 4 + u, last) * 8
                        here = pl.ds(pl.multiple_of(here, 8), GRAIN // 2)
                        for k in range(width):
                            best[k] = jnp.maximum(best[k], cols[k, here, :])
                    return tuple(best)

                low = jnp.full((GRAIN // 2, tokens), -3.0, jnp.float32)
                best = lax.fori_loop(0, (last + 4) // 4, widest, (low,) * width)
                for k in range(width):
                    peaks[k, seat : seat + 1, :] = jnp.max(best[k], axis=0, keepdims=True)

    seats = 4 * members
    seat = lax.broadcasted_iota(jnp.int32, (seats, 1), 0)
    recall = jnp.zeros((seats, LANES), jnp.float32)
    fresh = jnp.zeros((seats, LANES), jnp.int32)
    side_here = jnp.zeros((seats, 1), jnp.int32)
    side_came = jnp.zeros((seats, 1), jnp.int32)
    for i in range(members):
        mine = seat == 2 * members + i
        side_here = jnp.where(mine, side_now[i].astype(jnp.int32), side_here)
        side_came = jnp.where(mine, side_new[i].astype(jnp.int32), side_came)
    for k in range(slots):
        j = k % members
        length = far_len[j] if k < members else side_len[j]
        summed = jnp.sum(jnp.where(token < length, peaks[k], 0.0), axis=1, keepdims=True)
        recall = jnp.where(lane == k, summed / length.astype(jnp.float32), recall)
        if k < members:
            new, here = far_new[j].astype(jnp.int32), far_now[j].astype(jnp.int32)
            flag = jnp.where(seat < 2 * members, new, here * side_here * jnp.maximum(new, side_came))
        else:
            flag = jnp.where(seat < members, side_new[j].astype(jnp.int32), 0)
        fresh = jnp.where(lane == k, flag, fresh)
    precision = totals[...]
    score = 2.0 * precision * recall / jnp.maximum(precision + recall, 0.5)
    past = past_ref[...] if has_past else jnp.zeros((seats, LANES), jnp.float32)
    out_ref[...] = jnp.where(fresh > 0, score, past)


def score(members, before, own, twin, sides, fars, past=None):
    pieces = len(fars)
    count, width = own.shape
    tokens = (count - HEAD) // members
    operands = [own, twin, *sides, *fars] + ([] if past is None else [past])
    return pl.pallas_call(
        functools.partial(score_kernel, pieces, before, members, past is not None),
        out_shape=(
            jax.ShapeDtypeStruct((4 * members, LANES), jnp.float32),
            jax.ShapeDtypeStruct((3,), jnp.int32),
        ),
        in_specs=[pl.BlockSpec(memory_space=pltpu.VMEM)] * len(operands),
        out_specs=[
            pl.BlockSpec(memory_space=pltpu.VMEM),
            pl.BlockSpec(memory_space=pltpu.SMEM),
        ],
        scratch_shapes=[
            pltpu.VMEM((count, width), own.dtype),
            pltpu.VMEM((2 * members, tokens, width), own.dtype),
            pltpu.VMEM((2 * members, 3 * count // 2, tokens), jnp.float32),
            pltpu.VMEM((3 * count, LANES), jnp.float32),
            pltpu.VMEM((4 * members, LANES), jnp.float32),
            pltpu.VMEM((2 * members, 4 * members, tokens), jnp.float32),
            pltpu.SemaphoreType.DMA((pieces,)),
        ],
        compiler_params=pltpu.CompilerParams(vmem_limit_bytes=SCORE_VMEM),
        cost_estimate=pl.CostEstimate(
            flops=16 * count * count * width, bytes_accessed=8 * count * width, transcendentals=0
        ),
        name="score",
    )(*operands)


def assemble_kernel(place_ref, own_ref, twin_ref, side_ref, far_ref, pairs_ref, mean_ref):
    members = pairs_ref.shape[0]
    size = own_ref.shape[0]
    held = jnp.concatenate(
        [side_ref[...], far_ref[...], jnp.zeros((LANES - 2 * size, LANES), jnp.float32)], axis=0
    )
    odd = place_ref[0] == 1
    second = place_ref[1] == 1
    turned = held.T
    lane = lax.broadcasted_iota(jnp.int32, (members, LANES), 1)

    def straight(ref, k):
        return ref[k * members : (k + 1) * members, :]

    def across(which, k, j):
        first = which * size + k * members
        return pltpu.roll(turned[j * members : (j + 1) * members, :], (LANES - first) % LANES, 1)

    one, four = pltpu.roll(straight(own_ref, 0), LANES - members, 1), straight(side_ref, 2)
    two, three = across(0, 0, 1), across(1, 2, 0)
    five, six = straight(own_ref, 0), straight(twin_ref, 1)
    seven, eight = across(1, 0, 0), across(1, 1, 0)

    def join(same, other):
        low = jnp.where(second, other, same)
        high = pltpu.roll(jnp.where(second, same, other), members, 1)
        return jnp.where(lane < members, low, jnp.where(lane < 2 * members, high, 0.0))

    pick = lambda a, b: jnp.where(odd, b, a)
    parts = [
        [join(pick(one, four), pick(two, three)), join(pick(three, two), pick(four, one))],
        [join(pick(five, seven), pick(six, eight)), join(pick(seven, five), pick(eight, six))],
    ]
    total = jnp.zeros((members, LANES), jnp.float32)
    for r in range(2):
        for d in range(2):
            total = total + parts[r][d]
            for i in range(members):
                pairs_ref[i, r, d : d + 1, :] = parts[r][d][i : i + 1, : 2 * members]
    mean = jnp.sum(total, axis=1, keepdims=True) / (8.0 * members)
    diagonal = lane == lax.broadcasted_iota(jnp.int32, (members, LANES), 0)
    mean_ref[...] = jnp.sum(jnp.where(diagonal, mean, 0.0), axis=0, keepdims=True)[:, :members]


def assemble(place, own, twin, side, far, members):
    return pl.pallas_call(
        assemble_kernel,
        out_shape=(
            jax.ShapeDtypeStruct((members, 2, 2, 2 * members), jnp.float32),
            jax.ShapeDtypeStruct((1, members), jnp.float32),
        ),
        in_specs=[pl.BlockSpec(memory_space=pltpu.SMEM)] + [pl.BlockSpec(memory_space=pltpu.VMEM)] * 4,
        out_specs=[pl.BlockSpec(memory_space=pltpu.VMEM)] * 2,
        compiler_params=pltpu.CompilerParams(vmem_limit_bytes=4 * 1024 * 1024),
        name="assemble",
    )(place, own, twin, side, far)


def on_device(embeddings, lengths):
    members, tokens, _ = embeddings.shape
    blocks, cores = lax.axis_size("blk"), lax.axis_size("split")
    axes = ("blk", "split")
    far_path, side_path = z_route(blocks), x_route(blocks)
    twin_path = [(0, 1), (1, 0)]
    count = HEAD + members * tokens
    one = HEAD + members * tokens // 2 // GRAIN * GRAIN
    most = HEAD + members * tokens * 25 // 32 // GRAIN * GRAIN

    place = jnp.stack([lax.axis_index("blk") % 2, lax.axis_index("split")]).astype(jnp.int32)
    packed, first, second = pack(embeddings, lengths, one, most - one)
    side_one = lax.ppermute(first, axes, side_path)
    far_one = lax.ppermute(first, axes, far_path)
    side_two = lax.ppermute(second, axes, side_path)
    far_two = lax.ppermute(second, axes, far_path)
    twin = lax.ppermute(packed, "split", twin_path)

    early, needs = score(members, 0, packed, twin, [side_one], [far_one])

    sides, fars = [side_one, side_two], [far_one, far_two]
    late = score(members, one, packed, twin, sides, fars, early)[0]

    def long(late):
        rest = packed[most:]
        ahead = needs > most

        def fetch(route, colour, incoming):
            got = jnp.zeros_like(rest)
            for turn in range(2):
                pairs = [pair for pair in route if colour(pair[0] // 2, pair[0] % 2) == turn]
                sends = colour(lax.axis_index("blk"), lax.axis_index("split")) == turn
                arrived = lambda got: jnp.where(sends, got, lax.ppermute(rest, axes, pairs))
                used = jnp.where(sends, ahead[0], incoming)
                got = lax.cond(used, arrived, lambda got: got, got)
            return got

        side_rest = fetch(side_path, lambda b, s: b % 2, ahead[1])
        far_rest = fetch(far_path, lambda b, s: b // 2 % 2, ahead[2])
        return score(
            members, most, packed, twin, sides + [side_rest], fars + [far_rest], late
        )[0]

    scores = lax.cond(jnp.max(needs) > most, long, lambda late: late, late)
    side_scores = lax.ppermute(scores, axes, back(side_path))
    far_scores = lax.ppermute(scores, axes, back(far_path))
    twin_scores = lax.ppermute(scores, "split", twin_path)
    pair_f1, utility = assemble(place, scores, twin_scores, side_scores, far_scores, members)
    return (pair_f1, utility.reshape(members))


def solution(mesh):
    placed = (P(("group", "blk", "split"), None, None), P(("group", "blk", "split")))
    return jax.shard_map(
        on_device,
        mesh=mesh,
        in_specs=placed,
        out_specs=(P(("group", "blk", "split"), None, None, None), P(("group", "blk", "split"))),
        check_vma=False,
    )
```

```python
import functools
import jax
import jax.numpy as jnp
from jax import lax
from jax.experimental import pallas as pl
from jax.experimental.pallas import tpu as pltpu
from jax.sharding import PartitionSpec as P

GRAIN = 16
TILE = 256
UNROLLS = (8, 4, 2)
CUTS = (32, 48)
LANES = 128
HEAD = GRAIN
VMEM_LIMIT = 56 * 1024 * 1024
SCORE_VMEM = 28 * 1024 * 1024


def z_route(blocks):
    hop = lambda b: (b - 2) % blocks if b % 2 == 0 else (b + 2) % blocks
    return [(b * 2 + s, hop(b) * 2 + s) for b in range(blocks) for s in range(2)]


def x_route(blocks):
    hop = lambda b, s: (b + 1, 1 - s) if b % 2 == 0 else (b - 1, s)
    return [(b * 2 + s, hop(b, s)[0] * 2 + hop(b, s)[1]) for b in range(blocks) for s in range(2)]


def back(route):
    return [(target, source) for source, target in route]


def grains(length):
    return (length + (GRAIN - 1)) // GRAIN


def starts_of(lengths):
    starts = [jnp.int32(HEAD // GRAIN)]
    for length in lengths:
        starts.append(starts[-1] + grains(length))
    return starts


def pack_kernel(lengths_hbm, embeds_hbm, packed_hbm, *refs):
    parts, (lengths, embeds, packed, sems) = refs[:-4], refs[-4:]
    members, tokens, width = embeds_hbm.shape
    told = pltpu.make_async_copy(lengths_hbm, lengths, sems.at[members])
    told.start()
    loads = [
        pltpu.make_async_copy(embeds_hbm.at[i], embeds.at[i], sems.at[i]) for i in range(members)
    ]
    for load in loads:
        load.start()
    told.wait()
    row = lax.broadcasted_iota(jnp.int32, (HEAD, width), 0)
    head = jnp.zeros((HEAD, width), jnp.float32)
    for i in range(members):
        head = jnp.where(row == i, lengths[i].astype(jnp.float32), head)
    packed[0:HEAD, :] = head.astype(packed.dtype)
    starts = starts_of([lengths[i] for i in range(members)])
    token = lax.broadcasted_iota(jnp.int32, (tokens, 1), 0)
    for i in range(members):
        loads[i].wait()
        values = embeds[i].astype(jnp.float32)
        inverse = lax.rsqrt(jnp.mean(values * values, axis=-1, keepdims=True) + 1e-06)
        unit = values * inverse * width ** (-0.5)
        unit = jnp.where(token < lengths[i], unit, unit[0:1])
        first = pl.multiple_of(starts[i] * GRAIN, GRAIN)
        packed[pl.ds(first, tokens), :] = unit.astype(packed.dtype)
    stores, at = [], 0
    for k, part in enumerate(parts):
        size = part.shape[0]
        stores.append(pltpu.make_async_copy(packed.at[at : at + size], part, sems.at[k]))
        at += size
    stores.append(pltpu.make_async_copy(packed, packed_hbm, sems.at[members]))
    for store in stores:
        store.start()
    for store in stores:
        store.wait()


def pack(embeddings, lengths, cuts):
    members, tokens, width = embeddings.shape
    count = HEAD + members * tokens
    sizes = [count] + [b - a for a, b in zip([0] + cuts, cuts)]
    return pl.pallas_call(
        pack_kernel,
        out_shape=[jax.ShapeDtypeStruct((size, width), embeddings.dtype) for size in sizes],
        in_specs=[pl.BlockSpec(memory_space=pl.ANY)] * 2,
        out_specs=[pl.BlockSpec(memory_space=pl.ANY)] * len(sizes),
        scratch_shapes=[
            pltpu.SMEM((members,), jnp.int32),
            pltpu.VMEM((members, tokens, width), embeddings.dtype),
            pltpu.VMEM((count, width), embeddings.dtype),
            pltpu.SemaphoreType.DMA((members + 1,)),
        ],
        compiler_params=pltpu.CompilerParams(vmem_limit_bytes=VMEM_LIMIT),
        name="pack",
    )(lengths, embeddings)


def score_kernel(pieces, before, most, members, has_past, *refs):
    own, fars, sides = refs[0], refs[1 : 1 + pieces], refs[1 + pieces : 1 + 2 * pieces]
    twin_any = refs[1 + 2 * pieces]
    refs = refs[2 + 2 * pieces :]
    past_ref = refs[0] if has_past else None
    out_ref, over_ref, any_ref, twin, *scratch = refs[int(has_past) :]
    later, (sems, wide, cols, rows, totals, peaks) = scratch[:-6], scratch[-6:]
    count = own.shape[0]
    tokens = (count - HEAD) // members
    now = sum(piece.shape[0] for piece in fars)

    copies = [
        pltpu.make_async_copy(piece, target, sems.at[k])
        for k, (piece, target) in enumerate(zip((*fars[1:], *sides[1:]), later))
    ]
    quarter = count // 4 // GRAIN * GRAIN
    bounds = [0, quarter, 2 * quarter, 3 * quarter, count]
    twin_copies = [
        pltpu.make_async_copy(twin_any.at[a:b], twin.at[a:b], sems.at[2 * pieces - 1 + k])
        for k, (a, b) in enumerate(zip(bounds, bounds[1:]))
    ]
    for copy in copies + twin_copies:
        copy.start()
    fars = [fars[0], *later[: pieces - 1]]
    sides = [sides[0], *later[pieces - 1 :]]
    for copy in copies:
        copy.wait()

    def lengths_of(ref):
        head = ref[0:HEAD, 0:LANES].astype(jnp.float32)
        return [jnp.max(head[i : i + 1, :]).astype(jnp.int32) for i in range(members)]

    own_len, side_len, far_len = lengths_of(own), lengths_of(sides[0]), lengths_of(fars[0])
    own_start, side_start, far_start = starts_of(own_len), starts_of(side_len), starts_of(far_len)
    for k, start in enumerate((own_start, side_start, far_start)):
        over_ref[k] = (start[-1] * GRAIN > most).astype(jnp.int32)
    any_ref[0] = jnp.maximum(over_ref[0], jnp.maximum(over_ref[1], over_ref[2]))

    def state(start):
        ends = [start[i + 1] * GRAIN for i in range(members)]
        return [end <= now for end in ends], [end <= before for end in ends]

    side_now, side_old = state(side_start)
    far_now, far_old = state(far_start)
    side_new = [jnp.logical_and(a, jnp.logical_not(b)) for a, b in zip(side_now, side_old)]
    far_new = [jnp.logical_and(a, jnp.logical_not(b)) for a, b in zip(far_now, far_old)]

    def tiles(start):
        return ((start[-1] - HEAD // GRAIN) * GRAIN + (TILE - 1)) // TILE

    own_tiles = tiles(own_start)
    side_end = jnp.int32(HEAD // GRAIN)
    side_from = jnp.int32(HEAD // GRAIN)
    for i in range(members):
        side_end = jnp.where(side_now[i], side_start[i + 1], side_end)
        side_from = jnp.where(side_old[i], side_start[i + 1], side_from)
    side_tiles = ((side_end - HEAD // GRAIN) * GRAIN + (TILE - 1)) // TILE
    side_first = jnp.where(
        side_end > side_from, (side_from - HEAD // GRAIN) * GRAIN // TILE, side_tiles
    )
    slots = 2 * members
    zero = jnp.int32(0)

    def pick(refs, first):
        at, found = 0, None
        for ref in refs:
            size = ref.shape[0]
            here = jnp.clip(first - at, 0, size - GRAIN)
            rows = ref[pl.ds(pl.multiple_of(here, GRAIN), GRAIN), :]
            found = rows if found is None else jnp.where(first >= at, rows, found)
            at += size
        return found

    used = []
    for j in range(members):
        used.append(jnp.logical_and(far_now[j], jnp.logical_or(far_new[j], side_end > side_from)))
    used += side_new
    for k in range(slots):
        source, start, lengths = (
            (fars, far_start, far_len) if k < members else (sides, side_start, side_len)
        )
        j = k % members

        @pl.when(used[k])
        def _(k=k, j=j, source=source, start=start, lengths=lengths):
            for g in range(tokens // GRAIN):
                here = jnp.where(g * GRAIN < lengths[j], start[j] + g, start[j])
                wide[k, g * GRAIN : (g + 1) * GRAIN, :] = pick(source, here * GRAIN)

    lane = lax.broadcasted_iota(jnp.int32, (1, LANES), 1)

    def sweep(left, head, base, begins, ends):
        sums = [zero]
        for begin, end in zip(begins, ends):
            sums.append(sums[-1] + end - begin)
        total = sums[-1]

        def place_of(t):
            t = jnp.minimum(t, total - 1)
            slot, local = zero, t + begins[0]
            for k in range(1, len(begins)):
                slot = jnp.where(t >= sums[k], k, slot)
                local = jnp.where(t >= sums[k], t - sums[k] + begins[k], local)
            return slot, head + local * TILE

        def step(n, carry, offset, unroll):
            places = [place_of(offset + n * unroll + u) for u in range(unroll)]
            found = []
            for slot, first in places:
                part = left[pl.ds(pl.multiple_of(first, GRAIN), TILE), :]
                found.append(
                    lax.dot_general(
                        part,
                        wide[slot],
                        (((1,), (1,)), ((), ())),
                        preferred_element_type=jnp.float32,
                    )
                )
            for (slot, first), similar in zip(places, found):
                folded = similar.reshape(TILE // GRAIN, 2, GRAIN // 2, tokens)
                folded = jnp.max(folded, axis=1).reshape(TILE // 2, tokens)
                here = pl.ds(pl.multiple_of((base + first) // 2, GRAIN // 2), TILE // 2)
                cols[slot, here, :] = folded
                best = jnp.max(similar, axis=1, keepdims=True)
                here = pl.ds(pl.multiple_of(base + first, GRAIN), TILE)
                rows[here, :] = jnp.where(lane == slot, best, rows[here, :])
            return carry

        done = zero
        for unroll in UNROLLS[int(has_past) :]:
            rest = total - done
            turns = (rest if unroll > UNROLLS[-1] else rest + unroll - 1) // unroll
            lax.fori_loop(0, turns, functools.partial(step, offset=done, unroll=unroll), 0)
            done = done + turns * unroll

    far_own = [jnp.where(new, own_tiles, 0) for new in far_new]
    side_own = [jnp.where(new, own_tiles, 0) for new in side_new]
    sweep(own, HEAD, 0, [zero] * slots, far_own + side_own)
    for copy in twin_copies:
        copy.wait()
    twin_len = lengths_of(twin)
    twin_start = starts_of(twin_len)
    twin_tiles = tiles(twin_start)
    sweep(twin, HEAD, count, [zero] * members, [jnp.where(new, twin_tiles, 0) for new in far_new])
    begins = [jnp.where(new, 0, side_first) for new in far_new]
    ends = [jnp.where(here, side_tiles, begin) for here, begin in zip(far_now, begins)]
    at = 0
    for piece in sides:
        size, head = piece.shape[0], HEAD if at == 0 else 0
        low, high = (at + head - HEAD) // TILE, (at + size - HEAD) // TILE
        some = [jnp.clip(begin, low, high) - low for begin in begins]
        upto = [jnp.clip(end, low, high) - low for end in ends]
        sweep(piece, head, 2 * count + at, some, upto)
        at += size

    token = lax.broadcasted_iota(jnp.int32, (1, tokens), 1)
    row = lax.broadcasted_iota(jnp.int32, (tokens, 1), 0)
    far_any, side_any = far_new[0], side_new[0]
    for j in range(1, members):
        far_any = jnp.logical_or(far_any, far_new[j])
        side_any = jnp.logical_or(side_any, side_new[j])
    lens, starts = (own_len, twin_len, side_len), (own_start, twin_start, side_start)
    for which in range(3):
        for i in range(members):
            needed = (
                jnp.logical_or(far_any, side_any),
                far_any,
                jnp.logical_or(far_any, side_new[i]),
            )[which]

            @pl.when(needed)
            def _(which=which, i=i):
                width = slots if which == 0 else members
                length = lens[which][i]
                seat = which * members + i
                first = which * count + starts[which][i] * GRAIN
                window = rows[pl.ds(pl.multiple_of(first, GRAIN), tokens), :]
                window = jnp.sum(jnp.where(row < length, window, 0.0), axis=0, keepdims=True)
                totals[seat : seat + 1, :] = window / length.astype(jnp.float32)
                last = grains(length) - 1

                def widest(n, best):
                    best = list(best)
                    for u in range(4):
                        here = first // 2 + jnp.minimum(n * 4 + u, last) * 8
                        here = pl.ds(pl.multiple_of(here, 8), GRAIN // 2)
                        for k in range(width):
                            best[k] = jnp.maximum(best[k], cols[k, here, :])
                    return tuple(best)

                low = jnp.full((GRAIN // 2, tokens), -3.0, jnp.float32)
                best = lax.fori_loop(0, (last + 4) // 4, widest, (low,) * width)
                for k in range(width):
                    peaks[k, seat : seat + 1, :] = jnp.max(best[k], axis=0, keepdims=True)

    seats = 4 * members
    seat = lax.broadcasted_iota(jnp.int32, (seats, 1), 0)
    recall = jnp.zeros((seats, LANES), jnp.float32)
    fresh = jnp.zeros((seats, LANES), jnp.int32)
    side_here = jnp.zeros((seats, 1), jnp.int32)
    side_came = jnp.zeros((seats, 1), jnp.int32)
    for i in range(members):
        mine = seat == 2 * members + i
        side_here = jnp.where(mine, side_now[i].astype(jnp.int32), side_here)
        side_came = jnp.where(mine, side_new[i].astype(jnp.int32), side_came)
    for k in range(slots):
        j = k % members
        length = far_len[j] if k < members else side_len[j]
        summed = jnp.sum(jnp.where(token < length, peaks[k], 0.0), axis=1, keepdims=True)
        recall = jnp.where(lane == k, summed / length.astype(jnp.float32), recall)
        if k < members:
            new, here = far_new[j].astype(jnp.int32), far_now[j].astype(jnp.int32)
            flag = jnp.where(seat < 2 * members, new, here * side_here * jnp.maximum(new, side_came))
        else:
            flag = jnp.where(seat < members, side_new[j].astype(jnp.int32), 0)
        fresh = jnp.where(lane == k, flag, fresh)
    precision = totals[...]
    score = 2.0 * precision * recall / jnp.maximum(precision + recall, 0.5)
    past = past_ref[...] if has_past else jnp.zeros((seats, LANES), jnp.float32)
    out_ref[...] = jnp.where(fresh > 0, score, past)


def score(members, before, most, own, twin, sides, fars, past=None):
    pieces = len(fars)
    count, width = own.shape
    tokens = (count - HEAD) // members
    vmem = pl.BlockSpec(memory_space=pltpu.VMEM)
    apart = [pl.BlockSpec(memory_space=pl.ANY)] * (pieces - 1)
    piece_specs = [vmem] + apart
    past = [] if past is None else [past]
    return pl.pallas_call(
        functools.partial(score_kernel, pieces, before, most, members, len(past) > 0),
        out_shape=(
            jax.ShapeDtypeStruct((4 * members, LANES), jnp.float32),
            jax.ShapeDtypeStruct((3,), jnp.int32),
            jax.ShapeDtypeStruct((1,), jnp.int32),
        ),
        in_specs=[vmem, *piece_specs, *piece_specs, pl.BlockSpec(memory_space=pl.ANY)]
        + [vmem] * len(past),
        out_specs=[vmem] + [pl.BlockSpec(memory_space=pltpu.SMEM)] * 2,
        scratch_shapes=[
            pltpu.VMEM((count, width), own.dtype),
            *[pltpu.VMEM(piece.shape, piece.dtype) for piece in (*fars[1:], *sides[1:])],
            pltpu.SemaphoreType.DMA((2 * pieces + 3,)),
            pltpu.VMEM((2 * members, tokens, width), own.dtype),
            pltpu.VMEM((2 * members, 3 * count // 2, tokens), jnp.float32),
            pltpu.VMEM((3 * count, LANES), jnp.float32),
            pltpu.VMEM((4 * members, LANES), jnp.float32),
            pltpu.VMEM((2 * members, 4 * members, tokens), jnp.float32),
        ],
        compiler_params=pltpu.CompilerParams(vmem_limit_bytes=SCORE_VMEM),
        cost_estimate=pl.CostEstimate(
            flops=16 * count * count * width, bytes_accessed=8 * count * width, transcendentals=0
        ),
        name="score",
    )(own, *fars, *sides, twin, *past)


def assemble_kernel(place_ref, own_ref, twin_ref, far_ref, side_ref, pairs_ref, mean_ref):
    members = pairs_ref.shape[0]
    size = own_ref.shape[0]
    held = jnp.concatenate(
        [side_ref[...], far_ref[...], jnp.zeros((LANES - 2 * size, LANES), jnp.float32)], axis=0
    )
    odd = place_ref[0] == 1
    second = place_ref[1] == 1
    turned = held.T
    lane = lax.broadcasted_iota(jnp.int32, (members, LANES), 1)

    def straight(ref, k):
        return ref[k * members : (k + 1) * members, :]

    def across(which, k, j):
        first = which * size + k * members
        return pltpu.roll(turned[j * members : (j + 1) * members, :], (LANES - first) % LANES, 1)

    one, four = pltpu.roll(straight(own_ref, 0), LANES - members, 1), straight(side_ref, 2)
    two, three = across(0, 0, 1), across(1, 2, 0)
    five, six = straight(own_ref, 0), straight(twin_ref, 1)
    seven, eight = across(1, 0, 0), across(1, 1, 0)

    def join(same, other):
        low = jnp.where(second, other, same)
        high = pltpu.roll(jnp.where(second, same, other), members, 1)
        return jnp.where(lane < members, low, jnp.where(lane < 2 * members, high, 0.0))

    pick = lambda a, b: jnp.where(odd, b, a)
    parts = [
        [join(pick(one, four), pick(two, three)), join(pick(three, two), pick(four, one))],
        [join(pick(five, seven), pick(six, eight)), join(pick(seven, five), pick(eight, six))],
    ]
    total = jnp.zeros((members, LANES), jnp.float32)
    for r in range(2):
        for d in range(2):
            total = total + parts[r][d]
            for i in range(members):
                pairs_ref[i, r, d : d + 1, :] = parts[r][d][i : i + 1, : 2 * members]
    mean = jnp.sum(total, axis=1, keepdims=True) / (8.0 * members)
    diagonal = lane == lax.broadcasted_iota(jnp.int32, (members, LANES), 0)
    mean_ref[...] = jnp.sum(jnp.where(diagonal, mean, 0.0), axis=0, keepdims=True)[:, :members]


def assemble(place, own, twin, side, far, members):
    return pl.pallas_call(
        assemble_kernel,
        out_shape=(
            jax.ShapeDtypeStruct((members, 2, 2, 2 * members), jnp.float32),
            jax.ShapeDtypeStruct((1, members), jnp.float32),
        ),
        in_specs=[pl.BlockSpec(memory_space=pltpu.SMEM)] + [pl.BlockSpec(memory_space=pltpu.VMEM)] * 4,
        out_specs=[pl.BlockSpec(memory_space=pltpu.VMEM)] * 2,
        compiler_params=pltpu.CompilerParams(vmem_limit_bytes=4 * 1024 * 1024),
        name="assemble",
    )(place, own, twin, far, side)


def on_device(embeddings, lengths):
    members, tokens, _ = embeddings.shape
    blocks, cores = lax.axis_size("blk"), lax.axis_size("split")
    axes = ("blk", "split")
    far_path, side_path = z_route(blocks), x_route(blocks)
    twin_path = [(0, 1), (1, 0)]
    cuts = [HEAD + members * tokens * part // 64 // TILE * TILE for part in CUTS]
    most = cuts[-1]

    place = jnp.stack([lax.axis_index("blk") % 2, lax.axis_index("split")]).astype(jnp.int32)
    packed, *parts = pack(embeddings, lengths, cuts)
    fars = [lax.ppermute(part, axes, far_path) for part in parts]
    sides = [lax.ppermute(part, axes, side_path) for part in parts]
    twin = lax.ppermute(packed, "split", twin_path)

    late, over, some = score(members, 0, most, packed, twin, sides[:1], fars[:1])
    for k in range(1, len(cuts)):
        late = score(
            members, cuts[k - 1], most, packed, twin, sides[: k + 1], fars[: k + 1], late
        )[0]

    def long(late):
        rest = packed[most:]
        ahead = over > 0

        def fetch(route, colour, incoming):
            got = jnp.zeros_like(rest)
            for turn in range(2):
                pairs = [pair for pair in route if colour(pair[0] // 2, pair[0] % 2) == turn]
                sends = colour(lax.axis_index("blk"), lax.axis_index("split")) == turn
                arrived = lambda got: jnp.where(sends, got, lax.ppermute(rest, axes, pairs))
                used = jnp.where(sends, ahead[0], incoming)
                got = lax.cond(used, arrived, lambda got: got, got)
            return got

        side_rest = fetch(side_path, lambda b, s: b % 2, ahead[1])
        far_rest = fetch(far_path, lambda b, s: b // 2 % 2, ahead[2])
        return score(
            members, most, most, packed, twin, sides + [side_rest], fars + [far_rest], late
        )[0]

    scores = lax.cond(some.reshape(()) > 0, long, lambda late: late, late)
    side_scores = lax.ppermute(scores, axes, back(side_path))
    far_scores = lax.ppermute(scores, axes, back(far_path))
    twin_scores = lax.ppermute(scores, "split", twin_path)
    pair_f1, utility = assemble(place, scores, twin_scores, side_scores, far_scores, members)
    return (pair_f1, utility.reshape(members))


def solution(mesh):
    placed = (P(("group", "blk", "split"), None, None), P(("group", "blk", "split")))
    return jax.shard_map(
        on_device,
        mesh=mesh,
        in_specs=placed,
        out_specs=(P(("group", "blk", "split"), None, None, None), P(("group", "blk", "split"))),
        check_vma=False,
    )
```

```python
import functools
import jax
import jax.numpy as jnp
from jax import lax
from jax.experimental import pallas as pl
from jax.experimental.pallas import tpu as pltpu
from jax.sharding import PartitionSpec as P

GRAIN = 16
TILE = 256
UNROLLS = (8, 4, 2)
CUTS = (32, 48)
LANES = 128
HEAD = GRAIN
VMEM_LIMIT = 56 * 1024 * 1024
SCORE_VMEM = 28 * 1024 * 1024


def z_route(blocks):
    hop = lambda b: (b - 2) % blocks if b % 2 == 0 else (b + 2) % blocks
    return [(b * 2 + s, hop(b) * 2 + s) for b in range(blocks) for s in range(2)]


def x_route(blocks):
    hop = lambda b, s: (b + 1, 1 - s) if b % 2 == 0 else (b - 1, s)
    return [(b * 2 + s, hop(b, s)[0] * 2 + hop(b, s)[1]) for b in range(blocks) for s in range(2)]


def back(route):
    return [(target, source) for source, target in route]


def grains(length):
    return (length + (GRAIN - 1)) // GRAIN


def starts_of(lengths):
    starts = [jnp.int32(HEAD // GRAIN)]
    for length in lengths:
        starts.append(starts[-1] + grains(length))
    return starts


def pack_kernel(lengths_hbm, embeds_hbm, packed_hbm, *refs):
    parts, (lengths, embeds, packed, sems) = refs[:-4], refs[-4:]
    members, tokens, width = embeds_hbm.shape
    told = pltpu.make_async_copy(lengths_hbm, lengths, sems.at[members])
    told.start()
    loads = [
        pltpu.make_async_copy(embeds_hbm.at[i], embeds.at[i], sems.at[i]) for i in range(members)
    ]
    for load in loads:
        load.start()
    told.wait()
    row = lax.broadcasted_iota(jnp.int32, (HEAD, width), 0)
    head = jnp.zeros((HEAD, width), jnp.float32)
    for i in range(members):
        head = jnp.where(row == i, lengths[i].astype(jnp.float32), head)
    packed[0:HEAD, :] = head.astype(packed.dtype)
    starts = starts_of([lengths[i] for i in range(members)])
    token = lax.broadcasted_iota(jnp.int32, (tokens, 1), 0)
    for i in range(members):
        loads[i].wait()
        values = embeds[i].astype(jnp.float32)
        inverse = lax.rsqrt(jnp.mean(values * values, axis=-1, keepdims=True) + 1e-06)
        unit = values * inverse * width ** (-0.5)
        unit = jnp.where(token < lengths[i], unit, unit[0:1])
        first = pl.multiple_of(starts[i] * GRAIN, GRAIN)
        packed[pl.ds(first, tokens), :] = unit.astype(packed.dtype)
    stores, at = [], 0
    for k, part in enumerate(parts):
        size = part.shape[0]
        stores.append(pltpu.make_async_copy(packed.at[at : at + size], part, sems.at[k]))
        at += size
    stores.append(pltpu.make_async_copy(packed, packed_hbm, sems.at[members]))
    for store in stores:
        store.start()
    for store in stores:
        store.wait()


def pack(embeddings, lengths, cuts):
    members, tokens, width = embeddings.shape
    count = HEAD + members * tokens
    sizes = [count] + [b - a for a, b in zip([0] + cuts, cuts)]
    return pl.pallas_call(
        pack_kernel,
        out_shape=[jax.ShapeDtypeStruct((size, width), embeddings.dtype) for size in sizes],
        in_specs=[pl.BlockSpec(memory_space=pl.ANY)] * 2,
        out_specs=[pl.BlockSpec(memory_space=pl.ANY)] * len(sizes),
        scratch_shapes=[
            pltpu.SMEM((members,), jnp.int32),
            pltpu.VMEM((members, tokens, width), embeddings.dtype),
            pltpu.VMEM((count, width), embeddings.dtype),
            pltpu.SemaphoreType.DMA((members + 1,)),
        ],
        compiler_params=pltpu.CompilerParams(vmem_limit_bytes=VMEM_LIMIT),
        name="pack",
    )(lengths, embeddings)


def score_kernel(pieces, before, most, members, *refs):
    own, fars, sides = refs[0], refs[1 : 1 + pieces], refs[1 + pieces : 1 + 2 * pieces]
    twin_any = refs[1 + 2 * pieces]
    refs = refs[2 + 2 * pieces :]
    past_ref, out_ref, over_ref, any_ref, twin, *scratch = refs
    later, (sems, wide, cols, rows, totals, peaks) = scratch[:-6], scratch[-6:]
    count = own.shape[0]
    tokens = (count - HEAD) // members
    now = sum(piece.shape[0] for piece in fars)

    copies = [
        pltpu.make_async_copy(piece, target, sems.at[k])
        for k, (piece, target) in enumerate(zip((*fars[1:], *sides[1:]), later))
    ]
    quarter = count // 4 // GRAIN * GRAIN
    bounds = [0, quarter, 2 * quarter, 3 * quarter, count]
    twin_copies = [
        pltpu.make_async_copy(twin_any.at[a:b], twin.at[a:b], sems.at[2 * pieces - 1 + k])
        for k, (a, b) in enumerate(zip(bounds, bounds[1:]))
    ]
    for copy in copies + twin_copies:
        copy.start()
    fars = [fars[0], *later[: pieces - 1]]
    sides = [sides[0], *later[pieces - 1 :]]
    for copy in copies:
        copy.wait()

    def lengths_of(ref):
        head = ref[0:HEAD, 0:LANES].astype(jnp.float32)
        return [jnp.max(head[i : i + 1, :]).astype(jnp.int32) for i in range(members)]

    own_len, side_len, far_len = lengths_of(own), lengths_of(sides[0]), lengths_of(fars[0])
    own_start, side_start, far_start = starts_of(own_len), starts_of(side_len), starts_of(far_len)
    for k, start in enumerate((own_start, side_start, far_start)):
        over_ref[k] = (start[-1] * GRAIN > most).astype(jnp.int32)
    any_ref[0] = jnp.maximum(over_ref[0], jnp.maximum(over_ref[1], over_ref[2]))

    def state(start):
        ends = [start[i + 1] * GRAIN for i in range(members)]
        return [end <= now for end in ends], [end <= before for end in ends]

    side_now, side_old = state(side_start)
    far_now, far_old = state(far_start)
    side_new = [jnp.logical_and(a, jnp.logical_not(b)) for a, b in zip(side_now, side_old)]
    far_new = [jnp.logical_and(a, jnp.logical_not(b)) for a, b in zip(far_now, far_old)]

    def tiles(start):
        return ((start[-1] - HEAD // GRAIN) * GRAIN + (TILE - 1)) // TILE

    own_tiles = tiles(own_start)
    side_end = jnp.int32(HEAD // GRAIN)
    side_from = jnp.int32(HEAD // GRAIN)
    for i in range(members):
        side_end = jnp.where(side_now[i], side_start[i + 1], side_end)
        side_from = jnp.where(side_old[i], side_start[i + 1], side_from)
    side_tiles = ((side_end - HEAD // GRAIN) * GRAIN + (TILE - 1)) // TILE
    side_first = jnp.where(
        side_end > side_from, (side_from - HEAD // GRAIN) * GRAIN // TILE, side_tiles
    )
    slots = 2 * members
    zero = jnp.int32(0)

    def pick(refs, first):
        at, found = 0, None
        for ref in refs:
            size = ref.shape[0]
            here = jnp.clip(first - at, 0, size - GRAIN)
            rows = ref[pl.ds(pl.multiple_of(here, GRAIN), GRAIN), :]
            found = rows if found is None else jnp.where(first >= at, rows, found)
            at += size
        return found

    used = []
    for j in range(members):
        used.append(jnp.logical_and(far_now[j], jnp.logical_or(far_new[j], side_end > side_from)))
    used += side_new
    for k in range(slots):
        source, start, lengths = (
            (fars, far_start, far_len) if k < members else (sides, side_start, side_len)
        )
        j = k % members

        @pl.when(used[k])
        def _(k=k, j=j, source=source, start=start, lengths=lengths):
            for g in range(tokens // GRAIN):
                here = jnp.where(g * GRAIN < lengths[j], start[j] + g, start[j])
                wide[k, g * GRAIN : (g + 1) * GRAIN, :] = pick(source, here * GRAIN)

    lane = lax.broadcasted_iota(jnp.int32, (1, LANES), 1)

    def sweep(left, head, base, begins, ends):
        sums = [zero]
        for begin, end in zip(begins, ends):
            sums.append(sums[-1] + end - begin)
        total = sums[-1]

        def place_of(t):
            t = jnp.minimum(t, total - 1)
            slot, local = zero, t + begins[0]
            for k in range(1, len(begins)):
                slot = jnp.where(t >= sums[k], k, slot)
                local = jnp.where(t >= sums[k], t - sums[k] + begins[k], local)
            return slot, head + local * TILE

        def step(n, carry, offset, unroll):
            places = [place_of(offset + n * unroll + u) for u in range(unroll)]
            found = []
            for slot, first in places:
                part = left[pl.ds(pl.multiple_of(first, GRAIN), TILE), :]
                found.append(
                    lax.dot_general(
                        part,
                        wide[slot],
                        (((1,), (1,)), ((), ())),
                        preferred_element_type=jnp.float32,
                    )
                )
            for (slot, first), similar in zip(places, found):
                folded = similar.reshape(TILE // GRAIN, 2, GRAIN // 2, tokens)
                folded = jnp.max(folded, axis=1).reshape(TILE // 2, tokens)
                here = pl.ds(pl.multiple_of((base + first) // 2, GRAIN // 2), TILE // 2)
                cols[slot, here, :] = folded
                best = jnp.max(similar, axis=1, keepdims=True)
                here = pl.ds(pl.multiple_of(base + first, GRAIN), TILE)
                rows[here, :] = jnp.where(lane == slot, best, rows[here, :])
            return carry

        done = zero
        for unroll in UNROLLS[int(before > 0) :]:
            rest = total - done
            turns = (rest if unroll > UNROLLS[-1] else rest + unroll - 1) // unroll
            lax.fori_loop(0, turns, functools.partial(step, offset=done, unroll=unroll), 0)
            done = done + turns * unroll

    far_own = [jnp.where(new, own_tiles, 0) for new in far_new]
    side_own = [jnp.where(new, own_tiles, 0) for new in side_new]
    sweep(own, HEAD, 0, [zero] * slots, far_own + side_own)
    for copy in twin_copies:
        copy.wait()
    twin_len = lengths_of(twin)
    twin_start = starts_of(twin_len)
    twin_tiles = tiles(twin_start)
    sweep(twin, HEAD, count, [zero] * members, [jnp.where(new, twin_tiles, 0) for new in far_new])
    begins = [jnp.where(new, 0, side_first) for new in far_new]
    ends = [jnp.where(here, side_tiles, begin) for here, begin in zip(far_now, begins)]
    at = 0
    for piece in sides:
        size, head = piece.shape[0], HEAD if at == 0 else 0
        low, high = (at + head - HEAD) // TILE, (at + size - HEAD) // TILE
        some = [jnp.clip(begin, low, high) - low for begin in begins]
        upto = [jnp.clip(end, low, high) - low for end in ends]
        sweep(piece, head, 2 * count + at, some, upto)
        at += size

    token = lax.broadcasted_iota(jnp.int32, (1, tokens), 1)
    row = lax.broadcasted_iota(jnp.int32, (tokens, 1), 0)
    far_any, side_any = far_new[0], side_new[0]
    for j in range(1, members):
        far_any = jnp.logical_or(far_any, far_new[j])
        side_any = jnp.logical_or(side_any, side_new[j])
    lens, starts = (own_len, twin_len, side_len), (own_start, twin_start, side_start)
    for which in range(3):
        for i in range(members):
            needed = (
                jnp.logical_or(far_any, side_any),
                far_any,
                jnp.logical_or(far_any, side_new[i]),
            )[which]

            @pl.when(needed)
            def _(which=which, i=i):
                width = slots if which == 0 else members
                length = lens[which][i]
                seat = which * members + i
                first = which * count + starts[which][i] * GRAIN
                window = rows[pl.ds(pl.multiple_of(first, GRAIN), tokens), :]
                window = jnp.sum(jnp.where(row < length, window, 0.0), axis=0, keepdims=True)
                totals[seat : seat + 1, :] = window / length.astype(jnp.float32)
                last = grains(length) - 1

                def widest(n, best):
                    best = list(best)
                    for u in range(4):
                        here = first // 2 + jnp.minimum(n * 4 + u, last) * 8
                        here = pl.ds(pl.multiple_of(here, 8), GRAIN // 2)
                        for k in range(width):
                            best[k] = jnp.maximum(best[k], cols[k, here, :])
                    return tuple(best)

                low = jnp.full((GRAIN // 2, tokens), -3.0, jnp.float32)
                best = lax.fori_loop(0, (last + 4) // 4, widest, (low,) * width)
                for k in range(width):
                    peaks[k, seat : seat + 1, :] = jnp.max(best[k], axis=0, keepdims=True)

    seats = 4 * members
    seat = lax.broadcasted_iota(jnp.int32, (seats, 1), 0)
    recall = jnp.zeros((seats, LANES), jnp.float32)
    fresh = jnp.zeros((seats, LANES), jnp.int32)
    side_here = jnp.zeros((seats, 1), jnp.int32)
    side_came = jnp.zeros((seats, 1), jnp.int32)
    for i in range(members):
        mine = seat == 2 * members + i
        side_here = jnp.where(mine, side_now[i].astype(jnp.int32), side_here)
        side_came = jnp.where(mine, side_new[i].astype(jnp.int32), side_came)
    for k in range(slots):
        j = k % members
        length = far_len[j] if k < members else side_len[j]
        summed = jnp.sum(jnp.where(token < length, peaks[k], 0.0), axis=1, keepdims=True)
        recall = jnp.where(lane == k, summed / length.astype(jnp.float32), recall)
        if k < members:
            new, here = far_new[j].astype(jnp.int32), far_now[j].astype(jnp.int32)
            flag = jnp.where(seat < 2 * members, new, here * side_here * jnp.maximum(new, side_came))
        else:
            flag = jnp.where(seat < members, side_new[j].astype(jnp.int32), 0)
        fresh = jnp.where(lane == k, flag, fresh)
    precision = totals[...]
    score = 2.0 * precision * recall / jnp.maximum(precision + recall, 0.5)
    out_ref[...] = jnp.where(fresh > 0, score, past_ref[...])


def score(members, before, most, own, twin, sides, fars, past):
    pieces = len(fars)
    count, width = own.shape
    tokens = (count - HEAD) // members
    vmem = pl.BlockSpec(memory_space=pltpu.VMEM)
    apart = [pl.BlockSpec(memory_space=pl.ANY)] * (pieces - 1)
    piece_specs = [vmem] + apart
    return pl.pallas_call(
        functools.partial(score_kernel, pieces, before, most, members),
        out_shape=(
            jax.ShapeDtypeStruct((4 * members, LANES), jnp.float32),
            jax.ShapeDtypeStruct((3,), jnp.int32),
            jax.ShapeDtypeStruct((1,), jnp.int32),
        ),
        in_specs=[vmem, *piece_specs, *piece_specs, pl.BlockSpec(memory_space=pl.ANY)]
        + [vmem],
        out_specs=[vmem] + [pl.BlockSpec(memory_space=pltpu.SMEM)] * 2,
        scratch_shapes=[
            pltpu.VMEM((count, width), own.dtype),
            *[pltpu.VMEM(piece.shape, piece.dtype) for piece in (*fars[1:], *sides[1:])],
            pltpu.SemaphoreType.DMA((2 * pieces + 3,)),
            pltpu.VMEM((2 * members, tokens, width), own.dtype),
            pltpu.VMEM((2 * members, 3 * count // 2, tokens), jnp.float32),
            pltpu.VMEM((3 * count, LANES), jnp.float32),
            pltpu.VMEM((4 * members, LANES), jnp.float32),
            pltpu.VMEM((2 * members, 4 * members, tokens), jnp.float32),
        ],
        compiler_params=pltpu.CompilerParams(vmem_limit_bytes=SCORE_VMEM),
        cost_estimate=pl.CostEstimate(
            flops=16 * count * count * width, bytes_accessed=8 * count * width, transcendentals=0
        ),
        name="score",
    )(own, *fars, *sides, twin, past)


def assemble_kernel(own_ref, twin_ref, far_ref, side_ref, pairs_ref, mean_ref):
    members = pairs_ref.shape[0]
    size = own_ref.shape[0]
    held = jnp.concatenate(
        [side_ref[...], far_ref[...], jnp.zeros((LANES - 2 * size, LANES), jnp.float32)], axis=0
    )
    odd = own_ref[size - 2 : size - 1, :] > 0.5
    second = own_ref[size - 1 : size, :] > 0.5
    turned = held.T
    lane = lax.broadcasted_iota(jnp.int32, (members, LANES), 1)

    def straight(ref, k):
        return ref[k * members : (k + 1) * members, :]

    def across(which, k, j):
        first = which * size + k * members
        return pltpu.roll(turned[j * members : (j + 1) * members, :], (LANES - first) % LANES, 1)

    one, four = pltpu.roll(straight(own_ref, 0), LANES - members, 1), straight(side_ref, 2)
    two, three = across(0, 0, 1), across(1, 2, 0)
    five, six = straight(own_ref, 0), straight(twin_ref, 1)
    seven, eight = across(1, 0, 0), across(1, 1, 0)

    def join(same, other):
        low = jnp.where(second, other, same)
        high = pltpu.roll(jnp.where(second, same, other), members, 1)
        return jnp.where(lane < members, low, jnp.where(lane < 2 * members, high, 0.0))

    pick = lambda a, b: jnp.where(odd, b, a)
    parts = [
        [join(pick(one, four), pick(two, three)), join(pick(three, two), pick(four, one))],
        [join(pick(five, seven), pick(six, eight)), join(pick(seven, five), pick(eight, six))],
    ]
    total = jnp.zeros((members, LANES), jnp.float32)
    for r in range(2):
        for d in range(2):
            total = total + parts[r][d]
            for i in range(members):
                pairs_ref[i, r, d : d + 1, :] = parts[r][d][i : i + 1, : 2 * members]
    mean = jnp.sum(total, axis=1, keepdims=True) / (8.0 * members)
    diagonal = lane == lax.broadcasted_iota(jnp.int32, (members, LANES), 0)
    mean_ref[...] = jnp.sum(jnp.where(diagonal, mean, 0.0), axis=0, keepdims=True)[:, :members]


def assemble(own, twin, side, far, members):
    return pl.pallas_call(
        assemble_kernel,
        out_shape=(
            jax.ShapeDtypeStruct((members, 2, 2, 2 * members), jnp.float32),
            jax.ShapeDtypeStruct((1, members), jnp.float32),
        ),
        in_specs=[pl.BlockSpec(memory_space=pltpu.VMEM)] * 4,
        out_specs=[pl.BlockSpec(memory_space=pltpu.VMEM)] * 2,
        compiler_params=pltpu.CompilerParams(vmem_limit_bytes=4 * 1024 * 1024),
        name="assemble",
    )(own, twin, far, side)


def on_device(embeddings, lengths):
    members, tokens, _ = embeddings.shape
    blocks, cores = lax.axis_size("blk"), lax.axis_size("split")
    axes = ("blk", "split")
    far_path, side_path = z_route(blocks), x_route(blocks)
    twin_path = [(0, 1), (1, 0)]
    cuts = [HEAD + members * tokens * part // 64 // TILE * TILE for part in CUTS]
    most = cuts[-1]

    place = jnp.stack([lax.axis_index("blk") % 2, lax.axis_index("split")]).astype(jnp.float32)
    stamp = jnp.zeros((4 * members, LANES), jnp.float32).at[4 * members - 2 :].set(place[:, None])
    packed, *parts = pack(embeddings, lengths, cuts)
    fars = [lax.ppermute(part, axes, far_path) for part in parts]
    sides = [lax.ppermute(part, axes, side_path) for part in parts]
    twin = lax.ppermute(packed, "split", twin_path)

    late, over, some = score(members, 0, most, packed, twin, sides[:1], fars[:1], stamp)
    for k in range(1, len(cuts)):
        late = score(
            members, cuts[k - 1], most, packed, twin, sides[: k + 1], fars[: k + 1], late
        )[0]

    def long(late):
        rest = packed[most:]
        ahead = over > 0

        def fetch(route, colour, incoming):
            got = jnp.zeros_like(rest)
            for turn in range(2):
                pairs = [pair for pair in route if colour(pair[0] // 2, pair[0] % 2) == turn]
                sends = colour(lax.axis_index("blk"), lax.axis_index("split")) == turn
                arrived = lambda got: jnp.where(sends, got, lax.ppermute(rest, axes, pairs))
                used = jnp.where(sends, ahead[0], incoming)
                got = lax.cond(used, arrived, lambda got: got, got)
            return got

        side_rest = fetch(side_path, lambda b, s: b % 2, ahead[1])
        far_rest = fetch(far_path, lambda b, s: b // 2 % 2, ahead[2])
        return score(
            members, most, most, packed, twin, sides + [side_rest], fars + [far_rest], late
        )[0]

    scores = lax.cond(some.reshape(()) > 0, long, lambda late: late, late)
    side_scores = lax.ppermute(scores, axes, back(side_path))
    far_scores = lax.ppermute(scores, axes, back(far_path))
    twin_scores = lax.ppermute(scores, "split", twin_path)
    pair_f1, utility = assemble(scores, twin_scores, side_scores, far_scores, members)
    return (pair_f1, utility.reshape(members))


def solution(mesh):
    placed = (P(("group", "blk", "split"), None, None), P(("group", "blk", "split")))
    return jax.shard_map(
        on_device,
        mesh=mesh,
        in_specs=placed,
        out_specs=(P(("group", "blk", "split"), None, None, None), P(("group", "blk", "split"))),
        check_vma=False,
    )
```

```python
import functools
import jax
import jax.numpy as jnp
from jax import lax
from jax.experimental import pallas as pl
from jax.experimental.pallas import tpu as pltpu
from jax.sharding import PartitionSpec as P

GRAIN = 16
TILE = 256
FIRST_BODIES = (12,6,4,2)
LATER_BODIES = (4, 2, 1)
CUTS = (32, 48)
LANES = 128
HEAD = GRAIN
VMEM_LIMIT = 56 * 1024 * 1024
SCORE_VMEM = 28 * 1024 * 1024


def z_route(blocks):
    hop = lambda b: (b - 2) % blocks if b % 2 == 0 else (b + 2) % blocks
    return [(b * 2 + s, hop(b) * 2 + s) for b in range(blocks) for s in range(2)]


def x_route(blocks):
    hop = lambda b, s: (b + 1, 1 - s) if b % 2 == 0 else (b - 1, s)
    return [(b * 2 + s, hop(b, s)[0] * 2 + hop(b, s)[1]) for b in range(blocks) for s in range(2)]


def back(route):
    return [(target, source) for source, target in route]


def grains(length):
    return (length + (GRAIN - 1)) // GRAIN


def starts_of(lengths):
    starts = [jnp.int32(HEAD // GRAIN)]
    for length in lengths:
        starts.append(starts[-1] + grains(length))
    return starts


def pack_kernel(lengths_hbm, embeds_hbm, packed_hbm, *refs):
    parts, (lengths, embeds, packed, sems) = refs[:-4], refs[-4:]
    members, tokens, width = embeds_hbm.shape
    told = pltpu.make_async_copy(lengths_hbm, lengths, sems.at[members])
    told.start()
    loads = [
        pltpu.make_async_copy(embeds_hbm.at[i], embeds.at[i], sems.at[i]) for i in range(members)
    ]
    for load in loads:
        load.start()
    told.wait()
    row = lax.broadcasted_iota(jnp.int32, (HEAD, width), 0)
    head = jnp.zeros((HEAD, width), jnp.float32)
    for i in range(members):
        head = jnp.where(row == i, lengths[i].astype(jnp.float32), head)
    packed[0:HEAD, :] = head.astype(packed.dtype)
    starts = starts_of([lengths[i] for i in range(members)])
    token = lax.broadcasted_iota(jnp.int32, (tokens, 1), 0)
    for i in range(members):
        loads[i].wait()
        values = embeds[i].astype(jnp.float32)
        inverse = lax.rsqrt(jnp.mean(values * values, axis=-1, keepdims=True) + 1e-06)
        unit = values * inverse * width ** (-0.5)
        unit = jnp.where(token < lengths[i], unit, unit[0:1])
        first = pl.multiple_of(starts[i] * GRAIN, GRAIN)
        packed[pl.ds(first, tokens), :] = unit.astype(packed.dtype)
    stores, at = [], 0
    for k, part in enumerate(parts):
        size = part.shape[0]
        stores.append(pltpu.make_async_copy(packed.at[at : at + size], part, sems.at[k]))
        at += size
    stores.append(pltpu.make_async_copy(packed, packed_hbm, sems.at[members]))
    for store in stores:
        store.start()
    for store in stores:
        store.wait()


def pack(embeddings, lengths, cuts):
    members, tokens, width = embeddings.shape
    count = HEAD + members * tokens
    sizes = [count] + [b - a for a, b in zip([0] + cuts, cuts)]
    return pl.pallas_call(
        pack_kernel,
        out_shape=[jax.ShapeDtypeStruct((size, width), embeddings.dtype) for size in sizes],
        in_specs=[pl.BlockSpec(memory_space=pl.ANY)] * 2,
        out_specs=[pl.BlockSpec(memory_space=pl.ANY)] * len(sizes),
        scratch_shapes=[
            pltpu.SMEM((members,), jnp.int32),
            pltpu.VMEM((members, tokens, width), embeddings.dtype),
            pltpu.VMEM((count, width), embeddings.dtype),
            pltpu.SemaphoreType.DMA((members + 1,)),
        ],
        compiler_params=pltpu.CompilerParams(vmem_limit_bytes=VMEM_LIMIT),
        name="pack",
    )(lengths, embeddings)


def score_kernel(pieces, before, most, members, *refs):
    own, fars, sides = refs[0], refs[1 : 1 + pieces], refs[1 + pieces : 1 + 2 * pieces]
    twin_any = refs[1 + 2 * pieces]
    refs = refs[2 + 2 * pieces :]
    past_ref, out_ref, over_ref, any_ref, twin, *scratch = refs
    later, (sems, wide, cols, rows, totals, peaks) = scratch[:-6], scratch[-6:]
    count = own.shape[0]
    tokens = (count - HEAD) // members
    now = sum(piece.shape[0] for piece in fars)

    copies = [
        pltpu.make_async_copy(piece, target, sems.at[k])
        for k, (piece, target) in enumerate(zip((*fars[1:], *sides[1:]), later))
    ]
    quarter = count // 4 // GRAIN * GRAIN
    bounds = [0, quarter, 2 * quarter, 3 * quarter, count]
    twin_copies = [
        pltpu.make_async_copy(twin_any.at[a:b], twin.at[a:b], sems.at[2 * pieces - 1 + k])
        for k, (a, b) in enumerate(zip(bounds, bounds[1:]))
    ]
    for copy in copies + twin_copies:
        copy.start()
    fars = [fars[0], *later[: pieces - 1]]
    sides = [sides[0], *later[pieces - 1 :]]
    for copy in copies:
        copy.wait()

    def lengths_of(ref):
        head = ref[0:HEAD, 0:LANES].astype(jnp.float32)
        return [head[i, 0].astype(jnp.int32) for i in range(members)]

    own_len, side_len, far_len = lengths_of(own), lengths_of(sides[0]), lengths_of(fars[0])
    own_start, side_start, far_start = starts_of(own_len), starts_of(side_len), starts_of(far_len)
    for k, start in enumerate((own_start, side_start, far_start)):
        over_ref[k] = (start[-1] * GRAIN > most).astype(jnp.int32)
    any_ref[0] = jnp.maximum(over_ref[0], jnp.maximum(over_ref[1], over_ref[2]))

    def state(start):
        ends = [start[i + 1] * GRAIN for i in range(members)]
        return [end <= now for end in ends], [end <= before for end in ends]

    side_now, side_old = state(side_start)
    far_now, far_old = state(far_start)
    side_new = [jnp.logical_and(a, jnp.logical_not(b)) for a, b in zip(side_now, side_old)]
    far_new = [jnp.logical_and(a, jnp.logical_not(b)) for a, b in zip(far_now, far_old)]

    def tiles(start):
        return ((start[-1] - HEAD // GRAIN) * GRAIN + (TILE - 1)) // TILE

    own_tiles = tiles(own_start)
    side_end = jnp.int32(HEAD // GRAIN)
    side_from = jnp.int32(HEAD // GRAIN)
    for i in range(members):
        side_end = jnp.where(side_now[i], side_start[i + 1], side_end)
        side_from = jnp.where(side_old[i], side_start[i + 1], side_from)
    side_tiles = ((side_end - HEAD // GRAIN) * GRAIN + (TILE - 1)) // TILE
    side_first = jnp.where(
        side_end > side_from, (side_from - HEAD // GRAIN) * GRAIN // TILE, side_tiles
    )
    slots = 2 * members
    zero = jnp.int32(0)

    def pick(refs, first):
        at, found = 0, None
        for ref in refs:
            size = ref.shape[0]
            here = jnp.clip(first - at, 0, size - GRAIN)
            rows = ref[pl.ds(pl.multiple_of(here, GRAIN), GRAIN), :]
            found = rows if found is None else jnp.where(first >= at, rows, found)
            at += size
        return found

    used = []
    for j in range(members):
        used.append(jnp.logical_and(far_now[j], jnp.logical_or(far_new[j], side_end > side_from)))
    used += side_new
    for k in range(slots):
        source, start, lengths = (
            (fars, far_start, far_len) if k < members else (sides, side_start, side_len)
        )
        j = k % members

        @pl.when(used[k])
        def _(k=k, j=j, source=source, start=start, lengths=lengths):
            for g in range(tokens // GRAIN):
                here = jnp.where(g * GRAIN < lengths[j], start[j] + g, start[j])
                wide[k, g * GRAIN : (g + 1) * GRAIN, :] = pick(source, here * GRAIN)

    lane = lax.broadcasted_iota(jnp.int32, (1, LANES), 1)

    def sweep(left, head, base, begins, ends):
        sums = [zero]
        for begin, end in zip(begins, ends):
            sums.append(sums[-1] + end - begin)
        total = sums[-1]

        def place_of(t):
            t = jnp.minimum(t, total - 1)
            slot, local = zero, t + begins[0]
            for k in range(1, len(begins)):
                slot = jnp.where(t >= sums[k], k, slot)
                local = jnp.where(t >= sums[k], t - sums[k] + begins[k], local)
            return slot, head + local * TILE

        def step(n, carry, offset, unroll):
            places = [place_of(offset + n * unroll + u) for u in range(unroll)]
            found = []
            for slot, first in places:
                part = left[pl.ds(pl.multiple_of(first, GRAIN), TILE), :]
                found.append(
                    lax.dot_general(
                        part,
                        wide[slot],
                        (((1,), (1,)), ((), ())),
                        preferred_element_type=jnp.float32,
                    )
                )
            for (slot, first), similar in zip(places, found):
                folded = similar.reshape(TILE // GRAIN, 2, GRAIN // 2, tokens)
                folded = jnp.max(folded, axis=1).reshape(TILE // 2, tokens)
                here = pl.ds(pl.multiple_of((base + first) // 2, GRAIN // 2), TILE // 2)
                cols[slot, here, :] = folded
                best = jnp.max(similar, axis=1, keepdims=True)
                here = pl.ds(pl.multiple_of(base + first, GRAIN), TILE)
                rows[here, :] = jnp.where(lane == slot, best, rows[here, :])
            return carry

        done = zero
        bodies = LATER_BODIES if before else FIRST_BODIES
        for unroll in bodies:
            rest = total - done
            turns = (rest if unroll > bodies[-1] else rest + unroll - 1) // unroll
            lax.fori_loop(0, turns, functools.partial(step, offset=done, unroll=unroll), 0)
            done = done + turns * unroll

    far_own = [jnp.where(new, own_tiles, 0) for new in far_new]
    side_own = [jnp.where(new, own_tiles, 0) for new in side_new]
    sweep(own, HEAD, 0, [zero] * slots, far_own + side_own)
    for copy in twin_copies:
        copy.wait()
    twin_len = lengths_of(twin)
    twin_start = starts_of(twin_len)
    twin_tiles = tiles(twin_start)
    sweep(twin, HEAD, count, [zero] * members, [jnp.where(new, twin_tiles, 0) for new in far_new])
    begins = [jnp.where(new, 0, side_first) for new in far_new]
    ends = [jnp.where(here, side_tiles, begin) for here, begin in zip(far_now, begins)]
    at = 0
    for piece in sides:
        size, head = piece.shape[0], HEAD if at == 0 else 0
        low, high = (at + head - HEAD) // TILE, (at + size - HEAD) // TILE
        some = [jnp.clip(begin, low, high) - low for begin in begins]
        upto = [jnp.clip(end, low, high) - low for end in ends]
        sweep(piece, head, 2 * count + at, some, upto)
        at += size

    token = lax.broadcasted_iota(jnp.int32, (1, tokens), 1)
    row = lax.broadcasted_iota(jnp.int32, (tokens, 1), 0)
    far_any, side_any = far_new[0], side_new[0]
    for j in range(1, members):
        far_any = jnp.logical_or(far_any, far_new[j])
        side_any = jnp.logical_or(side_any, side_new[j])
    lens, starts = (own_len, twin_len, side_len), (own_start, twin_start, side_start)
    x_any = far_any
    for new in side_new:
        x_any = jnp.logical_or(x_any, new)
    for which, needed in enumerate((jnp.logical_or(far_any, side_any), far_any, x_any)):

        @pl.when(needed)
        def _(which=which):
            width = slots if which == 0 else members
            for i in range(members):
                length = lens[which][i]
                seat = which * members + i
                first = which * count + starts[which][i] * GRAIN
                window = rows[pl.ds(pl.multiple_of(first, GRAIN), tokens), :]
                window = jnp.sum(jnp.where(row < length, window, 0.0), axis=0, keepdims=True)
                totals[seat : seat + 1, :] = window / length.astype(jnp.float32)
                last = grains(length) - 1
                best = [jnp.full((GRAIN // 2, tokens), -3.0, jnp.float32)] * width
                for g in range(tokens // GRAIN):
                    here = first // 2 + jnp.minimum(g, last) * 8
                    here = pl.ds(pl.multiple_of(here, 8), GRAIN // 2)
                    for k in range(width):
                        best[k] = jnp.maximum(best[k], cols[k, here, :])
                for k in range(width):
                    peaks[k, seat : seat + 1, :] = jnp.max(best[k], axis=0, keepdims=True)

    seats = 4 * members
    seat = lax.broadcasted_iota(jnp.int32, (seats, 1), 0)
    recall = jnp.zeros((seats, LANES), jnp.float32)
    fresh = jnp.zeros((seats, LANES), jnp.int32)
    side_here = jnp.zeros((seats, 1), jnp.int32)
    side_came = jnp.zeros((seats, 1), jnp.int32)
    for i in range(members):
        mine = seat == 2 * members + i
        side_here = jnp.where(mine, side_now[i].astype(jnp.int32), side_here)
        side_came = jnp.where(mine, side_new[i].astype(jnp.int32), side_came)
    for k in range(slots):
        j = k % members
        length = far_len[j] if k < members else side_len[j]
        summed = jnp.sum(jnp.where(token < length, peaks[k], 0.0), axis=1, keepdims=True)
        recall = jnp.where(lane == k, summed / length.astype(jnp.float32), recall)
        if k < members:
            new, here = far_new[j].astype(jnp.int32), far_now[j].astype(jnp.int32)
            flag = jnp.where(seat < 2 * members, new, here * side_here * jnp.maximum(new, side_came))
        else:
            flag = jnp.where(seat < members, side_new[j].astype(jnp.int32), 0)
        fresh = jnp.where(lane == k, flag, fresh)
    precision = totals[...]
    score = 2.0 * precision * recall / jnp.maximum(precision + recall, 0.5)
    out_ref[...] = jnp.where(fresh > 0, score, past_ref[...])


def score(members, before, most, own, twin, sides, fars, past):
    pieces = len(fars)
    count, width = own.shape
    tokens = (count - HEAD) // members
    vmem = pl.BlockSpec(memory_space=pltpu.VMEM)
    apart = [pl.BlockSpec(memory_space=pl.ANY)] * (pieces - 1)
    piece_specs = [vmem] + apart
    return pl.pallas_call(
        functools.partial(score_kernel, pieces, before, most, members),
        out_shape=(
            jax.ShapeDtypeStruct((4 * members, LANES), jnp.float32),
            jax.ShapeDtypeStruct((3,), jnp.int32),
            jax.ShapeDtypeStruct((1,), jnp.int32),
        ),
        in_specs=[vmem, *piece_specs, *piece_specs, pl.BlockSpec(memory_space=pl.ANY)]
        + [vmem],
        out_specs=[vmem] + [pl.BlockSpec(memory_space=pltpu.SMEM)] * 2,
        scratch_shapes=[
            pltpu.VMEM((count, width), own.dtype),
            *[pltpu.VMEM(piece.shape, piece.dtype) for piece in (*fars[1:], *sides[1:])],
            pltpu.SemaphoreType.DMA((2 * pieces + 3,)),
            pltpu.VMEM((2 * members, tokens, width), own.dtype),
            pltpu.VMEM((2 * members, 3 * count // 2, tokens), jnp.float32),
            pltpu.VMEM((3 * count, LANES), jnp.float32),
            pltpu.VMEM((4 * members, LANES), jnp.float32),
            pltpu.VMEM((2 * members, 4 * members, tokens), jnp.float32),
        ],
        compiler_params=pltpu.CompilerParams(vmem_limit_bytes=SCORE_VMEM),
        cost_estimate=pl.CostEstimate(
            flops=16 * count * count * width, bytes_accessed=8 * count * width, transcendentals=0
        ),
        name="score",
    )(own, *fars, *sides, twin, past)


def assemble_kernel(own_ref, twin_ref, far_ref, side_ref, pairs_ref, mean_ref):
    members = pairs_ref.shape[0]
    size = own_ref.shape[0]
    held = jnp.concatenate(
        [side_ref[...], far_ref[...], jnp.zeros((LANES - 2 * size, LANES), jnp.float32)], axis=0
    )
    odd = own_ref[size - 2 : size - 1, :] > 0.5
    second = own_ref[size - 1 : size, :] > 0.5
    turned = held.T
    lane = lax.broadcasted_iota(jnp.int32, (members, LANES), 1)

    def straight(ref, k):
        return ref[k * members : (k + 1) * members, :]

    def across(which, k, j):
        first = which * size + k * members
        return pltpu.roll(turned[j * members : (j + 1) * members, :], (LANES - first) % LANES, 1)

    one, four = pltpu.roll(straight(own_ref, 0), LANES - members, 1), straight(side_ref, 2)
    two, three = across(0, 0, 1), across(1, 2, 0)
    five, six = straight(own_ref, 0), straight(twin_ref, 1)
    seven, eight = across(1, 0, 0), across(1, 1, 0)

    def join(same, other):
        low = jnp.where(second, other, same)
        high = pltpu.roll(jnp.where(second, same, other), members, 1)
        return jnp.where(lane < members, low, jnp.where(lane < 2 * members, high, 0.0))

    pick = lambda a, b: jnp.where(odd, b, a)
    parts = [
        [join(pick(one, four), pick(two, three)), join(pick(three, two), pick(four, one))],
        [join(pick(five, seven), pick(six, eight)), join(pick(seven, five), pick(eight, six))],
    ]
    total = jnp.zeros((members, LANES), jnp.float32)
    for r in range(2):
        for d in range(2):
            total = total + parts[r][d]
            for i in range(members):
                pairs_ref[i, r, d : d + 1, :] = parts[r][d][i : i + 1, : 2 * members]
    mean = jnp.sum(total, axis=1, keepdims=True) / (8.0 * members)
    diagonal = lane == lax.broadcasted_iota(jnp.int32, (members, LANES), 0)
    mean_ref[...] = jnp.sum(jnp.where(diagonal, mean, 0.0), axis=0, keepdims=True)[:, :members]


def assemble(own, twin, side, far, members):
    return pl.pallas_call(
        assemble_kernel,
        out_shape=(
            jax.ShapeDtypeStruct((members, 2, 2, 2 * members), jnp.float32),
            jax.ShapeDtypeStruct((1, members), jnp.float32),
        ),
        in_specs=[pl.BlockSpec(memory_space=pltpu.VMEM)] * 4,
        out_specs=[pl.BlockSpec(memory_space=pltpu.VMEM)] * 2,
        compiler_params=pltpu.CompilerParams(vmem_limit_bytes=4 * 1024 * 1024),
        name="assemble",
    )(own, twin, far, side)


def on_device(embeddings, lengths):
    members, tokens, _ = embeddings.shape
    blocks, cores = lax.axis_size("blk"), lax.axis_size("split")
    axes = ("blk", "split")
    far_path, side_path = z_route(blocks), x_route(blocks)
    twin_path = [(0, 1), (1, 0)]
    cuts = [HEAD + members * tokens * part // 64 // TILE * TILE for part in CUTS]
    most = cuts[-1]

    place = jnp.stack([lax.axis_index("blk") % 2, lax.axis_index("split")]).astype(jnp.float32)
    stamp = jnp.zeros((4 * members, LANES), jnp.float32).at[4 * members - 2 :].set(place[:, None])
    packed, *parts = pack(embeddings, lengths, cuts)
    fars = [lax.ppermute(part, axes, far_path) for part in parts]
    sides = [lax.ppermute(part, axes, side_path) for part in parts]
    twin = lax.ppermute(packed, "split", twin_path)

    late, over, some = score(members, 0, most, packed, twin, sides[:1], fars[:1], stamp)
    for k in range(1, len(cuts)):
        late = score(
            members, cuts[k - 1], most, packed, twin, sides[: k + 1], fars[: k + 1], late
        )[0]

    def long(late):
        rest = packed[most:]
        ahead = over > 0

        def fetch(route, colour, incoming):
            got = jnp.zeros_like(rest)
            for turn in range(2):
                pairs = [pair for pair in route if colour(pair[0] // 2, pair[0] % 2) == turn]
                sends = colour(lax.axis_index("blk"), lax.axis_index("split")) == turn
                arrived = lambda got: jnp.where(sends, got, lax.ppermute(rest, axes, pairs))
                used = jnp.where(sends, ahead[0], incoming)
                got = lax.cond(used, arrived, lambda got: got, got)
            return got

        side_rest = fetch(side_path, lambda b, s: b % 2, ahead[1])
        far_rest = fetch(far_path, lambda b, s: b // 2 % 2, ahead[2])
        return score(
            members, most, most, packed, twin, sides + [side_rest], fars + [far_rest], late
        )[0]

    scores = lax.cond(some.reshape(()) > 0, long, lambda late: late, late)
    side_scores = lax.ppermute(scores, axes, back(side_path))
    far_scores = lax.ppermute(scores, axes, back(far_path))
    twin_scores = lax.ppermute(scores, "split", twin_path)
    pair_f1, utility = assemble(scores, twin_scores, side_scores, far_scores, members)
    return (pair_f1, utility.reshape(members))


def solution(mesh):
    placed = (P(("group", "blk", "split"), None, None), P(("group", "blk", "split")))
    return jax.shard_map(
        on_device,
        mesh=mesh,
        in_specs=placed,
        out_specs=(P(("group", "blk", "split"), None, None, None), P(("group", "blk", "split"))),
        check_vma=False,
    )
```

```python
import functools
import jax
import jax.numpy as jnp
from jax import lax
from jax.experimental import pallas as pl
from jax.experimental.pallas import tpu as pltpu
from jax.sharding import PartitionSpec as P

GRAIN = 16
TILE = 256
FIRST_BODIES = (12,6,4,2)
LATER_BODIES = (4, 2, 1)
CUTS = (32, 48)
LANES = 128
HEAD = GRAIN
VMEM_LIMIT = 56 * 1024 * 1024
SCORE_VMEM = 28 * 1024 * 1024


def z_route(blocks):
    hop = lambda b: (b - 2) % blocks if b % 2 == 0 else (b + 2) % blocks
    return [(b * 2 + s, hop(b) * 2 + s) for b in range(blocks) for s in range(2)]


def x_route(blocks):
    hop = lambda b, s: (b + 1, 1 - s) if b % 2 == 0 else (b - 1, s)
    return [(b * 2 + s, hop(b, s)[0] * 2 + hop(b, s)[1]) for b in range(blocks) for s in range(2)]


def back(route):
    return [(target, source) for source, target in route]


def grains(length):
    return (length + (GRAIN - 1)) // GRAIN


def starts_of(lengths):
    starts = [jnp.int32(HEAD // GRAIN)]
    for length in lengths:
        starts.append(starts[-1] + grains(length))
    return starts


def pack_kernel(lengths_hbm, embeds_hbm, packed_hbm, *refs):
    parts, (lengths, embeds, packed, sems) = refs[:-4], refs[-4:]
    members, tokens, width = embeds_hbm.shape
    told = pltpu.make_async_copy(lengths_hbm, lengths, sems.at[members])
    told.start()
    loads = [
        pltpu.make_async_copy(embeds_hbm.at[i], embeds.at[i], sems.at[i]) for i in range(members)
    ]
    for load in loads:
        load.start()
    told.wait()
    row = lax.broadcasted_iota(jnp.int32, (HEAD, width), 0)
    head = jnp.zeros((HEAD, width), jnp.float32)
    for i in range(members):
        head = jnp.where(row == i, lengths[i].astype(jnp.float32), head)
    packed[0:HEAD, :] = head.astype(packed.dtype)
    starts = starts_of([lengths[i] for i in range(members)])
    token = lax.broadcasted_iota(jnp.int32, (tokens, 1), 0)
    for i in range(members):
        loads[i].wait()
        values = embeds[i].astype(jnp.float32)
        inverse = lax.rsqrt(jnp.mean(values * values, axis=-1, keepdims=True) + 1e-06)
        unit = values * (inverse * width ** (-0.5))
        unit = jnp.where(token < lengths[i], unit, unit[0:1])
        first = pl.multiple_of(starts[i] * GRAIN, GRAIN)
        packed[pl.ds(first, tokens), :] = unit.astype(packed.dtype)
    stores, at = [], 0
    for k, part in enumerate(parts):
        size = part.shape[0]
        stores.append(pltpu.make_async_copy(packed.at[at : at + size], part, sems.at[k]))
        at += size
    stores.append(pltpu.make_async_copy(packed, packed_hbm, sems.at[members]))
    for store in stores:
        store.start()
    for store in stores:
        store.wait()


def pack(embeddings, lengths, cuts):
    members, tokens, width = embeddings.shape
    count = HEAD + members * tokens
    sizes = [count] + [b - a for a, b in zip([0] + cuts, cuts)]
    return pl.pallas_call(
        pack_kernel,
        out_shape=[jax.ShapeDtypeStruct((size, width), embeddings.dtype) for size in sizes],
        in_specs=[pl.BlockSpec(memory_space=pl.ANY)] * 2,
        out_specs=[pl.BlockSpec(memory_space=pl.ANY)] * len(sizes),
        scratch_shapes=[
            pltpu.SMEM((members,), jnp.int32),
            pltpu.VMEM((members, tokens, width), embeddings.dtype),
            pltpu.VMEM((count, width), embeddings.dtype),
            pltpu.SemaphoreType.DMA((members + 1,)),
        ],
        compiler_params=pltpu.CompilerParams(vmem_limit_bytes=VMEM_LIMIT),
        name="pack",
    )(lengths, embeddings)


def score_kernel(pieces, before, most, members, *refs):
    own, fars, sides = refs[0], refs[1 : 1 + pieces], refs[1 + pieces : 1 + 2 * pieces]
    twin_any = refs[1 + 2 * pieces]
    refs = refs[2 + 2 * pieces :]
    past_ref, out_ref, over_ref, any_ref, twin, *scratch = refs
    later, (sems, wide, cols, rows, totals, peaks) = scratch[:-6], scratch[-6:]
    count = own.shape[0]
    tokens = (count - HEAD) // members
    now = sum(piece.shape[0] for piece in fars)

    copies = [
        pltpu.make_async_copy(piece, target, sems.at[k])
        for k, (piece, target) in enumerate(zip((*fars[1:], *sides[1:]), later))
    ]
    quarter = count // 4 // GRAIN * GRAIN
    bounds = [0, quarter, 2 * quarter, 3 * quarter, count]
    twin_copies = [
        pltpu.make_async_copy(twin_any.at[a:b], twin.at[a:b], sems.at[2 * pieces - 1 + k])
        for k, (a, b) in enumerate(zip(bounds, bounds[1:]))
    ]
    for copy in copies if before else twin_copies:
        copy.start()
    fars = [fars[0], *later[: pieces - 1]]
    sides = [sides[0], *later[pieces - 1 :]]
    for copy in copies:
        copy.wait()
    if before:
        for copy in twin_copies:
            copy.start()

    def lengths_of(ref):
        head = ref[0:HEAD, 0:LANES].astype(jnp.float32)
        return [head[i, 0].astype(jnp.int32) for i in range(members)]

    own_len, side_len, far_len = lengths_of(own), lengths_of(sides[0]), lengths_of(fars[0])
    own_start, side_start, far_start = starts_of(own_len), starts_of(side_len), starts_of(far_len)
    for k, start in enumerate((own_start, side_start, far_start)):
        over_ref[k] = (start[-1] * GRAIN > most).astype(jnp.int32)
    any_ref[0] = jnp.maximum(over_ref[0], jnp.maximum(over_ref[1], over_ref[2]))

    def state(start):
        ends = [start[i + 1] * GRAIN for i in range(members)]
        return [end <= now for end in ends], [end <= before for end in ends]

    side_now, side_old = state(side_start)
    far_now, far_old = state(far_start)
    side_new = [jnp.logical_and(a, jnp.logical_not(b)) for a, b in zip(side_now, side_old)]
    far_new = [jnp.logical_and(a, jnp.logical_not(b)) for a, b in zip(far_now, far_old)]

    def tiles(start):
        return ((start[-1] - HEAD // GRAIN) * GRAIN + (TILE - 1)) // TILE

    own_tiles = tiles(own_start)
    side_end = jnp.int32(HEAD // GRAIN)
    side_from = jnp.int32(HEAD // GRAIN)
    for i in range(members):
        side_end = jnp.where(side_now[i], side_start[i + 1], side_end)
        side_from = jnp.where(side_old[i], side_start[i + 1], side_from)
    side_tiles = ((side_end - HEAD // GRAIN) * GRAIN + (TILE - 1)) // TILE
    side_first = jnp.where(
        side_end > side_from, (side_from - HEAD // GRAIN) * GRAIN // TILE, side_tiles
    )
    slots = 2 * members
    zero = jnp.int32(0)

    def pick(refs, first):
        at, found = 0, None
        for ref in refs:
            size = ref.shape[0]
            here = jnp.clip(first - at, 0, size - GRAIN)
            rows = ref[pl.ds(pl.multiple_of(here, GRAIN), GRAIN), :]
            found = rows if found is None else jnp.where(first >= at, rows, found)
            at += size
        return found

    used = []
    for j in range(members):
        used.append(jnp.logical_and(far_now[j], jnp.logical_or(far_new[j], side_end > side_from)))
    used += side_new
    for k in range(slots):
        source, start, lengths = (
            (fars, far_start, far_len) if k < members else (sides, side_start, side_len)
        )
        j = k % members

        @pl.when(used[k])
        def _(k=k, j=j, source=source, start=start, lengths=lengths):
            for g in range(tokens // GRAIN):
                here = jnp.where(g * GRAIN < lengths[j], start[j] + g, start[j])
                wide[k, g * GRAIN : (g + 1) * GRAIN, :] = pick(source, here * GRAIN)

    lane = lax.broadcasted_iota(jnp.int32, (1, LANES), 1)

    def sweep(left, head, base, begins, ends):
        sums = [zero]
        for begin, end in zip(begins, ends):
            sums.append(sums[-1] + end - begin)
        total = sums[-1]

        def place_of(t):
            t = jnp.minimum(t, total - 1)
            slot, local = zero, t + begins[0]
            for k in range(1, len(begins)):
                slot = jnp.where(t >= sums[k], k, slot)
                local = jnp.where(t >= sums[k], t - sums[k] + begins[k], local)
            return slot, head + local * TILE

        def step(n, carry, offset, unroll):
            places = [place_of(offset + n * unroll + u) for u in range(unroll)]
            found = []
            for slot, first in places:
                part = left[pl.ds(pl.multiple_of(first, GRAIN), TILE), :]
                found.append(
                    lax.dot_general(
                        part,
                        wide[slot],
                        (((1,), (1,)), ((), ())),
                        preferred_element_type=jnp.float32,
                    )
                )
            for (slot, first), similar in zip(places, found):
                folded = similar.reshape(TILE // GRAIN, 2, GRAIN // 2, tokens)
                folded = jnp.max(folded, axis=1).reshape(TILE // 2, tokens)
                here = pl.ds(pl.multiple_of((base + first) // 2, GRAIN // 2), TILE // 2)
                cols[slot, here, :] = folded
                best = jnp.max(similar, axis=1, keepdims=True)
                here = pl.ds(pl.multiple_of(base + first, GRAIN), TILE)
                rows[here, :] = jnp.where(lane == slot, best, rows[here, :])
            return carry

        done = zero
        bodies = LATER_BODIES if before else FIRST_BODIES
        for unroll in bodies:
            rest = total - done
            turns = (rest if unroll > bodies[-1] else rest + unroll - 1) // unroll
            lax.fori_loop(0, turns, functools.partial(step, offset=done, unroll=unroll), 0)
            done = done + turns * unroll

    far_own = [jnp.where(new, own_tiles, 0) for new in far_new]
    side_own = [jnp.where(new, own_tiles, 0) for new in side_new]
    sweep(own, HEAD, 0, [zero] * slots, far_own + side_own)
    for copy in twin_copies:
        copy.wait()
    twin_len = lengths_of(twin)
    twin_start = starts_of(twin_len)
    twin_tiles = tiles(twin_start)
    sweep(twin, HEAD, count, [zero] * members, [jnp.where(new, twin_tiles, 0) for new in far_new])
    begins = [jnp.where(new, 0, side_first) for new in far_new]
    ends = [jnp.where(here, side_tiles, begin) for here, begin in zip(far_now, begins)]
    at = 0
    for piece in sides:
        size, head = piece.shape[0], HEAD if at == 0 else 0
        low, high = (at + head - HEAD) // TILE, (at + size - HEAD) // TILE
        some = [jnp.clip(begin, low, high) - low for begin in begins]
        upto = [jnp.clip(end, low, high) - low for end in ends]
        sweep(piece, head, 2 * count + at, some, upto)
        at += size

    token = lax.broadcasted_iota(jnp.int32, (1, tokens), 1)
    row = lax.broadcasted_iota(jnp.int32, (tokens, 1), 0)
    far_any, side_any = far_new[0], side_new[0]
    for j in range(1, members):
        far_any = jnp.logical_or(far_any, far_new[j])
        side_any = jnp.logical_or(side_any, side_new[j])
    lens, starts = (own_len, twin_len, side_len), (own_start, twin_start, side_start)
    x_any = far_any
    for new in side_new:
        x_any = jnp.logical_or(x_any, new)
    for which, needed in enumerate((jnp.logical_or(far_any, side_any), far_any, x_any)):

        @pl.when(needed)
        def _(which=which):
            width = slots if which == 0 else members
            for i in range(members):
                length = lens[which][i]
                seat = which * members + i
                first = which * count + starts[which][i] * GRAIN
                window = rows[pl.ds(pl.multiple_of(first, GRAIN), tokens), :]
                window = jnp.sum(jnp.where(row < length, window, 0.0), axis=0, keepdims=True)
                totals[seat : seat + 1, :] = window / length.astype(jnp.float32)
                last = grains(length) - 1
                best = [jnp.full((GRAIN // 2, tokens), -3.0, jnp.float32)] * width
                for g in range(tokens // GRAIN):
                    here = first // 2 + jnp.minimum(g, last) * 8
                    here = pl.ds(pl.multiple_of(here, 8), GRAIN // 2)
                    for k in range(width):
                        best[k] = jnp.maximum(best[k], cols[k, here, :])
                for k in range(width):
                    peaks[k, seat : seat + 1, :] = jnp.max(best[k], axis=0, keepdims=True)

    seats = 4 * members
    seat = lax.broadcasted_iota(jnp.int32, (seats, 1), 0)
    recall = jnp.zeros((seats, LANES), jnp.float32)
    fresh = jnp.zeros((seats, LANES), jnp.int32)
    side_here = jnp.zeros((seats, 1), jnp.int32)
    side_came = jnp.zeros((seats, 1), jnp.int32)
    for i in range(members):
        mine = seat == 2 * members + i
        side_here = jnp.where(mine, side_now[i].astype(jnp.int32), side_here)
        side_came = jnp.where(mine, side_new[i].astype(jnp.int32), side_came)
    for k in range(slots):
        j = k % members
        length = far_len[j] if k < members else side_len[j]
        summed = jnp.sum(jnp.where(token < length, peaks[k], 0.0), axis=1, keepdims=True)
        recall = jnp.where(lane == k, summed / length.astype(jnp.float32), recall)
        if k < members:
            new, here = far_new[j].astype(jnp.int32), far_now[j].astype(jnp.int32)
            flag = jnp.where(seat < 2 * members, new, here * side_here * jnp.maximum(new, side_came))
        else:
            flag = jnp.where(seat < members, side_new[j].astype(jnp.int32), 0)
        fresh = jnp.where(lane == k, flag, fresh)
    precision = totals[...]
    score = 2.0 * precision * recall / jnp.maximum(precision + recall, 0.5)
    out_ref[...] = jnp.where(fresh > 0, score, past_ref[...])


def score(members, before, most, own, twin, sides, fars, past):
    pieces = len(fars)
    count, width = own.shape
    tokens = (count - HEAD) // members
    vmem = pl.BlockSpec(memory_space=pltpu.VMEM)
    apart = [pl.BlockSpec(memory_space=pl.ANY)] * (pieces - 1)
    piece_specs = [vmem] + apart
    return pl.pallas_call(
        functools.partial(score_kernel, pieces, before, most, members),
        out_shape=(
            jax.ShapeDtypeStruct((4 * members, LANES), jnp.float32),
            jax.ShapeDtypeStruct((3,), jnp.int32),
            jax.ShapeDtypeStruct((1,), jnp.int32),
        ),
        in_specs=[vmem, *piece_specs, *piece_specs, pl.BlockSpec(memory_space=pl.ANY)]
        + [vmem],
        out_specs=[vmem] + [pl.BlockSpec(memory_space=pltpu.SMEM)] * 2,
        scratch_shapes=[
            pltpu.VMEM((count, width), own.dtype),
            *[pltpu.VMEM(piece.shape, piece.dtype) for piece in (*fars[1:], *sides[1:])],
            pltpu.SemaphoreType.DMA((2 * pieces + 3,)),
            pltpu.VMEM((2 * members, tokens, width), own.dtype),
            pltpu.VMEM((2 * members, 3 * count // 2, tokens), jnp.float32),
            pltpu.VMEM((3 * count, LANES), jnp.float32),
            pltpu.VMEM((4 * members, LANES), jnp.float32),
            pltpu.VMEM((2 * members, 4 * members, tokens), jnp.float32),
        ],
        compiler_params=pltpu.CompilerParams(vmem_limit_bytes=SCORE_VMEM),
        cost_estimate=pl.CostEstimate(
            flops=16 * count * count * width, bytes_accessed=8 * count * width, transcendentals=0
        ),
        name="score",
    )(own, *fars, *sides, twin, past)


def assemble_kernel(own_ref, twin_ref, far_ref, side_ref, pairs_ref, mean_ref):
    members = pairs_ref.shape[0]
    size = own_ref.shape[0]
    held = jnp.concatenate(
        [side_ref[...], far_ref[...], jnp.zeros((LANES - 2 * size, LANES), jnp.float32)], axis=0
    )
    odd = own_ref[size - 2 : size - 1, :] > 0.5
    second = own_ref[size - 1 : size, :] > 0.5
    turned = held.T
    lane = lax.broadcasted_iota(jnp.int32, (members, LANES), 1)

    def straight(ref, k):
        return ref[k * members : (k + 1) * members, :]

    def across(which, k, j):
        first = which * size + k * members
        return pltpu.roll(turned[j * members : (j + 1) * members, :], (LANES - first) % LANES, 1)

    one, four = pltpu.roll(straight(own_ref, 0), LANES - members, 1), straight(side_ref, 2)
    two, three = across(0, 0, 1), across(1, 2, 0)
    five, six = straight(own_ref, 0), straight(twin_ref, 1)
    seven, eight = across(1, 0, 0), across(1, 1, 0)

    def join(same, other):
        low = jnp.where(second, other, same)
        high = pltpu.roll(jnp.where(second, same, other), members, 1)
        return jnp.where(lane < members, low, jnp.where(lane < 2 * members, high, 0.0))

    pick = lambda a, b: jnp.where(odd, b, a)
    parts = [
        [join(pick(one, four), pick(two, three)), join(pick(three, two), pick(four, one))],
        [join(pick(five, seven), pick(six, eight)), join(pick(seven, five), pick(eight, six))],
    ]
    total = jnp.zeros((members, LANES), jnp.float32)
    for r in range(2):
        for d in range(2):
            total = total + parts[r][d]
            for i in range(members):
                pairs_ref[i, r, d : d + 1, :] = parts[r][d][i : i + 1, : 2 * members]
    mean = jnp.sum(total, axis=1, keepdims=True) / (8.0 * members)
    diagonal = lane == lax.broadcasted_iota(jnp.int32, (members, LANES), 0)
    mean_ref[...] = jnp.sum(jnp.where(diagonal, mean, 0.0), axis=0, keepdims=True)[:, :members]


def assemble(own, twin, side, far, members):
    return pl.pallas_call(
        assemble_kernel,
        out_shape=(
            jax.ShapeDtypeStruct((members, 2, 2, 2 * members), jnp.float32),
            jax.ShapeDtypeStruct((1, members), jnp.float32),
        ),
        in_specs=[pl.BlockSpec(memory_space=pltpu.VMEM)] * 4,
        out_specs=[pl.BlockSpec(memory_space=pltpu.VMEM)] * 2,
        compiler_params=pltpu.CompilerParams(vmem_limit_bytes=4 * 1024 * 1024),
        name="assemble",
    )(own, twin, far, side)


def on_device(embeddings, lengths):
    members, tokens, _ = embeddings.shape
    blocks, cores = lax.axis_size("blk"), lax.axis_size("split")
    axes = ("blk", "split")
    far_path, side_path = z_route(blocks), x_route(blocks)
    twin_path = [(0, 1), (1, 0)]
    cuts = [HEAD + members * tokens * part // 64 // TILE * TILE for part in CUTS]
    most = cuts[-1]

    place = jnp.stack([lax.axis_index("blk") % 2, lax.axis_index("split")]).astype(jnp.float32)
    stamp = jnp.zeros((4 * members, LANES), jnp.float32).at[4 * members - 2 :].set(place[:, None])
    packed, *parts = pack(embeddings, lengths, cuts)
    fars = [lax.ppermute(part, axes, far_path) for part in parts]
    sides = [lax.ppermute(part, axes, side_path) for part in parts]
    twin = lax.ppermute(packed, "split", twin_path)

    late, over, some = score(members, 0, most, packed, twin, sides[:1], fars[:1], stamp)
    for k in range(1, len(cuts)):
        late = score(
            members, cuts[k - 1], most, packed, twin, sides[: k + 1], fars[: k + 1], late
        )[0]

    def long(late):
        rest = packed[most:]
        ahead = over > 0

        def fetch(route, colour, incoming):
            got = jnp.zeros_like(rest)
            for turn in range(2):
                pairs = [pair for pair in route if colour(pair[0] // 2, pair[0] % 2) == turn]
                sends = colour(lax.axis_index("blk"), lax.axis_index("split")) == turn
                arrived = lambda got: jnp.where(sends, got, lax.ppermute(rest, axes, pairs))
                used = jnp.where(sends, ahead[0], incoming)
                got = lax.cond(used, arrived, lambda got: got, got)
            return got

        side_rest = fetch(side_path, lambda b, s: b % 2, ahead[1])
        far_rest = fetch(far_path, lambda b, s: b // 2 % 2, ahead[2])
        return score(
            members, most, most, packed, twin, sides + [side_rest], fars + [far_rest], late
        )[0]

    scores = lax.cond(some.reshape(()) > 0, long, lambda late: late, late)
    side_scores = lax.ppermute(scores, axes, back(side_path))
    far_scores = lax.ppermute(scores, axes, back(far_path))
    twin_scores = lax.ppermute(scores, "split", twin_path)
    pair_f1, utility = assemble(scores, twin_scores, side_scores, far_scores, members)
    return (pair_f1, utility.reshape(members))


def solution(mesh):
    placed = (P(("group", "blk", "split"), None, None), P(("group", "blk", "split")))
    return jax.shard_map(
        on_device,
        mesh=mesh,
        in_specs=placed,
        out_specs=(P(("group", "blk", "split"), None, None, None), P(("group", "blk", "split"))),
        check_vma=False,
    )
```

```python
import functools
import jax
import jax.numpy as jnp
from jax import lax
from jax.experimental import pallas as pl
from jax.experimental.pallas import tpu as pltpu
from jax.sharding import PartitionSpec as P

GRAIN = 16
TILE = 256
FIRST_BODIES = (8, 6, 4, 2)
LATER_BODIES = (6, 4, 2, 1)
CUTS = (32, 48)
LANES = 128
HEAD = GRAIN
VMEM_LIMIT = 56 * 1024 * 1024
SCORE_VMEM = 28 * 1024 * 1024


def z_route(blocks):
    hop = lambda b: (b - 2) % blocks if b % 2 == 0 else (b + 2) % blocks
    return [(b * 2 + s, hop(b) * 2 + s) for b in range(blocks) for s in range(2)]


def x_route(blocks):
    hop = lambda b, s: (b + 1, 1 - s) if b % 2 == 0 else (b - 1, s)
    return [(b * 2 + s, hop(b, s)[0] * 2 + hop(b, s)[1]) for b in range(blocks) for s in range(2)]


def back(route):
    return [(target, source) for source, target in route]


def grains(length):
    return (length + (GRAIN - 1)) // GRAIN


def starts_of(lengths):
    starts = [jnp.int32(HEAD // GRAIN)]
    for length in lengths:
        starts.append(starts[-1] + grains(length))
    return starts


def pack_kernel(lengths_hbm, embeds_hbm, packed_hbm, *refs):
    parts, (lengths, embeds, packed, sems) = refs[:-4], refs[-4:]
    members, tokens, width = embeds_hbm.shape
    told = pltpu.make_async_copy(lengths_hbm, lengths, sems.at[members])
    told.start()
    loads = [
        pltpu.make_async_copy(embeds_hbm.at[i], embeds.at[i], sems.at[i]) for i in range(members)
    ]
    for load in loads:
        load.start()
    told.wait()
    row = lax.broadcasted_iota(jnp.int32, (HEAD, width), 0)
    head = jnp.zeros((HEAD, width), jnp.float32)
    for i in range(members):
        head = jnp.where(row == i, lengths[i].astype(jnp.float32), head)
    packed[0:HEAD, :] = head.astype(packed.dtype)
    starts = starts_of([lengths[i] for i in range(members)])
    token = lax.broadcasted_iota(jnp.int32, (tokens, 1), 0)
    for i in range(members):
        loads[i].wait()
        values = embeds[i].astype(jnp.float32)
        inverse = lax.rsqrt(jnp.mean(values * values, axis=-1, keepdims=True) + 1e-06)
        unit = values * inverse * width ** (-0.5)
        unit = jnp.where(token < lengths[i], unit, unit[0:1])
        first = pl.multiple_of(starts[i] * GRAIN, GRAIN)
        packed[pl.ds(first, tokens), :] = unit.astype(packed.dtype)
    stores, at = [], 0
    for k, part in enumerate(parts):
        size = part.shape[0]
        stores.append(pltpu.make_async_copy(packed.at[at : at + size], part, sems.at[k]))
        at += size
    stores.append(pltpu.make_async_copy(packed, packed_hbm, sems.at[members]))
    for store in stores:
        store.start()
    for store in stores:
        store.wait()


def pack(embeddings, lengths, cuts):
    members, tokens, width = embeddings.shape
    count = HEAD + members * tokens
    sizes = [count] + [b - a for a, b in zip([0] + cuts, cuts)]
    return pl.pallas_call(
        pack_kernel,
        out_shape=[jax.ShapeDtypeStruct((size, width), embeddings.dtype) for size in sizes],
        in_specs=[pl.BlockSpec(memory_space=pl.ANY)] * 2,
        out_specs=[pl.BlockSpec(memory_space=pl.ANY)] * len(sizes),
        scratch_shapes=[
            pltpu.SMEM((members,), jnp.int32),
            pltpu.VMEM((members, tokens, width), embeddings.dtype),
            pltpu.VMEM((count, width), embeddings.dtype),
            pltpu.SemaphoreType.DMA((members + 1,)),
        ],
        compiler_params=pltpu.CompilerParams(vmem_limit_bytes=VMEM_LIMIT),
        name="pack",
    )(lengths, embeddings)


def score_kernel(pieces, before, most, members, *refs):
    own, fars, sides = refs[0], refs[1 : 1 + pieces], refs[1 + pieces : 1 + 2 * pieces]
    twin_any = refs[1 + 2 * pieces]
    refs = refs[2 + 2 * pieces :]
    past_ref, out_ref, over_ref, any_ref, twin, *scratch = refs
    later, (sems, wide, cols, rows, totals, peaks) = scratch[:-6], scratch[-6:]
    count = own.shape[0]
    tokens = (count - HEAD) // members
    now = sum(piece.shape[0] for piece in fars)

    copies = [
        pltpu.make_async_copy(piece, target, sems.at[k])
        for k, (piece, target) in enumerate(zip((*fars[1:], *sides[1:]), later))
    ]
    quarter = count // 4 // GRAIN * GRAIN
    bounds = [0, quarter, 2 * quarter, 3 * quarter, count]
    twin_copies = [
        pltpu.make_async_copy(twin_any.at[a:b], twin.at[a:b], sems.at[2 * pieces - 1 + k])
        for k, (a, b) in enumerate(zip(bounds, bounds[1:]))
    ]
    for copy in copies + twin_copies:
        copy.start()
    fars = [fars[0], *later[: pieces - 1]]
    sides = [sides[0], *later[pieces - 1 :]]
    for copy in copies:
        copy.wait()

    def lengths_of(ref):
        head = ref[0:HEAD, 0:LANES].astype(jnp.float32)
        return [head[i, 0].astype(jnp.int32) for i in range(members)]

    own_len, side_len, far_len = lengths_of(own), lengths_of(sides[0]), lengths_of(fars[0])
    own_start, side_start, far_start = starts_of(own_len), starts_of(side_len), starts_of(far_len)
    for k, start in enumerate((own_start, side_start, far_start)):
        over_ref[k] = (start[-1] * GRAIN > most).astype(jnp.int32)
    any_ref[0] = jnp.maximum(over_ref[0], jnp.maximum(over_ref[1], over_ref[2]))

    def state(start):
        ends = [start[i + 1] * GRAIN for i in range(members)]
        return [end <= now for end in ends], [end <= before for end in ends]

    side_now, side_old = state(side_start)
    far_now, far_old = state(far_start)
    side_new = [jnp.logical_and(a, jnp.logical_not(b)) for a, b in zip(side_now, side_old)]
    far_new = [jnp.logical_and(a, jnp.logical_not(b)) for a, b in zip(far_now, far_old)]

    def tiles(start):
        return ((start[-1] - HEAD // GRAIN) * GRAIN + (TILE - 1)) // TILE

    own_tiles = tiles(own_start)
    side_end = jnp.int32(HEAD // GRAIN)
    side_from = jnp.int32(HEAD // GRAIN)
    for i in range(members):
        side_end = jnp.where(side_now[i], side_start[i + 1], side_end)
        side_from = jnp.where(side_old[i], side_start[i + 1], side_from)
    side_tiles = ((side_end - HEAD // GRAIN) * GRAIN + (TILE - 1)) // TILE
    side_first = jnp.where(
        side_end > side_from, (side_from - HEAD // GRAIN) * GRAIN // TILE, side_tiles
    )
    slots = 2 * members
    zero = jnp.int32(0)

    def pick(refs, first):
        at, found = 0, None
        for ref in refs:
            size = ref.shape[0]
            here = jnp.clip(first - at, 0, size - GRAIN)
            rows = ref[pl.ds(pl.multiple_of(here, GRAIN), GRAIN), :]
            found = rows if found is None else jnp.where(first >= at, rows, found)
            at += size
        return found

    used = []
    for j in range(members):
        used.append(jnp.logical_and(far_now[j], jnp.logical_or(far_new[j], side_end > side_from)))
    used += side_new
    for k in range(slots):
        source, start, lengths = (
            (fars, far_start, far_len) if k < members else (sides, side_start, side_len)
        )
        j = k % members

        @pl.when(used[k])
        def _(k=k, j=j, source=source, start=start, lengths=lengths):
            for g in range(tokens // GRAIN):
                here = jnp.where(g * GRAIN < lengths[j], start[j] + g, start[j])
                wide[k, g * GRAIN : (g + 1) * GRAIN, :] = pick(source, here * GRAIN)

    lane = lax.broadcasted_iota(jnp.int32, (1, LANES), 1)

    def sweep(left, head, base, begins, ends):
        sums = [zero]
        for begin, end in zip(begins, ends):
            sums.append(sums[-1] + end - begin)
        total = sums[-1]

        def place_of(t):
            t = jnp.minimum(t, total - 1)
            slot, local = zero, t + begins[0]
            for k in range(1, len(begins)):
                slot = jnp.where(t >= sums[k], k, slot)
                local = jnp.where(t >= sums[k], t - sums[k] + begins[k], local)
            return slot, head + local * TILE

        def step(n, carry, offset, unroll):
            places = [place_of(offset + n * unroll + u) for u in range(unroll)]
            found = []
            for slot, first in places:
                part = left[pl.ds(pl.multiple_of(first, GRAIN), TILE), :]
                found.append(
                    lax.dot_general(
                        part,
                        wide[slot],
                        (((1,), (1,)), ((), ())),
                        preferred_element_type=jnp.float32,
                    )
                )
            for (slot, first), similar in zip(places, found):
                folded = similar.reshape(TILE // GRAIN, 2, GRAIN // 2, tokens)
                folded = jnp.max(folded, axis=1).reshape(TILE // 2, tokens)
                here = pl.ds(pl.multiple_of((base + first) // 2, GRAIN // 2), TILE // 2)
                cols[slot, here, :] = folded
                best = jnp.max(similar, axis=1, keepdims=True)
                here = pl.ds(pl.multiple_of(base + first, GRAIN), TILE)
                rows[here, :] = jnp.where(lane == slot, best, rows[here, :])
            return carry

        done = zero
        bodies = LATER_BODIES if before else FIRST_BODIES
        for unroll in bodies:
            rest = total - done
            turns = (rest if unroll > bodies[-1] else rest + unroll - 1) // unroll
            lax.fori_loop(0, turns, functools.partial(step, offset=done, unroll=unroll), 0)
            done = done + turns * unroll

    far_own = [jnp.where(new, own_tiles, 0) for new in far_new]
    side_own = [jnp.where(new, own_tiles, 0) for new in side_new]
    sweep(own, HEAD, 0, [zero] * slots, far_own + side_own)
    for copy in twin_copies:
        copy.wait()
    twin_len = lengths_of(twin)
    twin_start = starts_of(twin_len)
    twin_tiles = tiles(twin_start)
    sweep(twin, HEAD, count, [zero] * members, [jnp.where(new, twin_tiles, 0) for new in far_new])
    begins = [jnp.where(new, 0, side_first) for new in far_new]
    ends = [jnp.where(here, side_tiles, begin) for here, begin in zip(far_now, begins)]
    at = 0
    for piece in sides:
        size, head = piece.shape[0], HEAD if at == 0 else 0
        low, high = (at + head - HEAD) // TILE, (at + size - HEAD) // TILE
        some = [jnp.clip(begin, low, high) - low for begin in begins]
        upto = [jnp.clip(end, low, high) - low for end in ends]
        sweep(piece, head, 2 * count + at, some, upto)
        at += size

    token = lax.broadcasted_iota(jnp.int32, (1, tokens), 1)
    row = lax.broadcasted_iota(jnp.int32, (tokens, 1), 0)
    far_any, side_any = far_new[0], side_new[0]
    for j in range(1, members):
        far_any = jnp.logical_or(far_any, far_new[j])
        side_any = jnp.logical_or(side_any, side_new[j])
    lens, starts = (own_len, twin_len, side_len), (own_start, twin_start, side_start)
    x_any = far_any
    for new in side_new:
        x_any = jnp.logical_or(x_any, new)
    for which, needed in enumerate((jnp.logical_or(far_any, side_any), far_any, x_any)):

        @pl.when(needed)
        def _(which=which):
            width = slots if which == 0 else members
            for i in range(members):
                length = lens[which][i]
                seat = which * members + i
                first = which * count + starts[which][i] * GRAIN
                window = rows[pl.ds(pl.multiple_of(first, GRAIN), tokens), :]
                window = jnp.sum(jnp.where(row < length, window, 0.0), axis=0, keepdims=True)
                totals[seat : seat + 1, :] = window / length.astype(jnp.float32)
                last = grains(length) - 1
                best = [jnp.full((GRAIN // 2, tokens), -3.0, jnp.float32)] * width
                for g in range(tokens // GRAIN):
                    here = first // 2 + jnp.minimum(g, last) * 8
                    here = pl.ds(pl.multiple_of(here, 8), GRAIN // 2)
                    for k in range(width):
                        best[k] = jnp.maximum(best[k], cols[k, here, :])
                for k in range(width):
                    peaks[k, seat : seat + 1, :] = jnp.max(best[k], axis=0, keepdims=True)

    seats = 4 * members
    seat = lax.broadcasted_iota(jnp.int32, (seats, 1), 0)
    recall = jnp.zeros((seats, LANES), jnp.float32)
    fresh = jnp.zeros((seats, LANES), jnp.int32)
    side_here = jnp.zeros((seats, 1), jnp.int32)
    side_came = jnp.zeros((seats, 1), jnp.int32)
    for i in range(members):
        mine = seat == 2 * members + i
        side_here = jnp.where(mine, side_now[i].astype(jnp.int32), side_here)
        side_came = jnp.where(mine, side_new[i].astype(jnp.int32), side_came)
    for k in range(slots):
        j = k % members
        length = far_len[j] if k < members else side_len[j]
        summed = jnp.sum(jnp.where(token < length, peaks[k], 0.0), axis=1, keepdims=True)
        recall = jnp.where(lane == k, summed / length.astype(jnp.float32), recall)
        if k < members:
            new, here = far_new[j].astype(jnp.int32), far_now[j].astype(jnp.int32)
            flag = jnp.where(seat < 2 * members, new, here * side_here * jnp.maximum(new, side_came))
        else:
            flag = jnp.where(seat < members, side_new[j].astype(jnp.int32), 0)
        fresh = jnp.where(lane == k, flag, fresh)
    precision = totals[...]
    score = 2.0 * precision * recall / jnp.maximum(precision + recall, 0.5)
    out_ref[...] = jnp.where(fresh > 0, score, past_ref[...])


def score(members, before, most, own, twin, sides, fars, past):
    pieces = len(fars)
    count, width = own.shape
    tokens = (count - HEAD) // members
    vmem = pl.BlockSpec(memory_space=pltpu.VMEM)
    apart = [pl.BlockSpec(memory_space=pl.ANY)] * (pieces - 1)
    piece_specs = [vmem] + apart
    return pl.pallas_call(
        functools.partial(score_kernel, pieces, before, most, members),
        out_shape=(
            jax.ShapeDtypeStruct((4 * members, LANES), jnp.float32),
            jax.ShapeDtypeStruct((3,), jnp.int32),
            jax.ShapeDtypeStruct((1,), jnp.int32),
        ),
        in_specs=[vmem, *piece_specs, *piece_specs, pl.BlockSpec(memory_space=pl.ANY)]
        + [vmem],
        out_specs=[vmem] + [pl.BlockSpec(memory_space=pltpu.SMEM)] * 2,
        scratch_shapes=[
            pltpu.VMEM((count, width), own.dtype),
            *[pltpu.VMEM(piece.shape, piece.dtype) for piece in (*fars[1:], *sides[1:])],
            pltpu.SemaphoreType.DMA((2 * pieces + 3,)),
            pltpu.VMEM((2 * members, tokens, width), own.dtype),
            pltpu.VMEM((2 * members, 3 * count // 2, tokens), jnp.float32),
            pltpu.VMEM((3 * count, LANES), jnp.float32),
            pltpu.VMEM((4 * members, LANES), jnp.float32),
            pltpu.VMEM((2 * members, 4 * members, tokens), jnp.float32),
        ],
        compiler_params=pltpu.CompilerParams(vmem_limit_bytes=SCORE_VMEM),
        cost_estimate=pl.CostEstimate(
            flops=16 * count * count * width, bytes_accessed=8 * count * width, transcendentals=0
        ),
        name="score",
    )(own, *fars, *sides, twin, past)


def assemble_kernel(own_ref, twin_ref, far_ref, side_ref, pairs_ref, mean_ref):
    members = pairs_ref.shape[0]
    size = own_ref.shape[0]
    held = jnp.concatenate(
        [side_ref[...], far_ref[...], jnp.zeros((LANES - 2 * size, LANES), jnp.float32)], axis=0
    )
    odd = own_ref[size - 2 : size - 1, :] > 0.5
    second = own_ref[size - 1 : size, :] > 0.5
    turned = held.T
    lane = lax.broadcasted_iota(jnp.int32, (members, LANES), 1)

    def straight(ref, k):
        return ref[k * members : (k + 1) * members, :]

    def across(which, k, j):
        first = which * size + k * members
        return pltpu.roll(turned[j * members : (j + 1) * members, :], (LANES - first) % LANES, 1)

    one, four = pltpu.roll(straight(own_ref, 0), LANES - members, 1), straight(side_ref, 2)
    two, three = across(0, 0, 1), across(1, 2, 0)
    five, six = straight(own_ref, 0), straight(twin_ref, 1)
    seven, eight = across(1, 0, 0), across(1, 1, 0)

    def join(same, other):
        low = jnp.where(second, other, same)
        high = pltpu.roll(jnp.where(second, same, other), members, 1)
        return jnp.where(lane < members, low, jnp.where(lane < 2 * members, high, 0.0))

    pick = lambda a, b: jnp.where(odd, b, a)
    parts = [
        [join(pick(one, four), pick(two, three)), join(pick(three, two), pick(four, one))],
        [join(pick(five, seven), pick(six, eight)), join(pick(seven, five), pick(eight, six))],
    ]
    total = jnp.zeros((members, LANES), jnp.float32)
    for r in range(2):
        for d in range(2):
            total = total + parts[r][d]
            for i in range(members):
                pairs_ref[i, r, d : d + 1, :] = parts[r][d][i : i + 1, : 2 * members]
    mean = jnp.sum(total, axis=1, keepdims=True) / (8.0 * members)
    diagonal = lane == lax.broadcasted_iota(jnp.int32, (members, LANES), 0)
    mean_ref[...] = jnp.sum(jnp.where(diagonal, mean, 0.0), axis=0, keepdims=True)[:, :members]


def assemble(own, twin, side, far, members):
    return pl.pallas_call(
        assemble_kernel,
        out_shape=(
            jax.ShapeDtypeStruct((members, 2, 2, 2 * members), jnp.float32),
            jax.ShapeDtypeStruct((1, members), jnp.float32),
        ),
        in_specs=[pl.BlockSpec(memory_space=pltpu.VMEM)] * 4,
        out_specs=[pl.BlockSpec(memory_space=pltpu.VMEM)] * 2,
        compiler_params=pltpu.CompilerParams(vmem_limit_bytes=4 * 1024 * 1024),
        name="assemble",
    )(own, twin, far, side)


def on_device(embeddings, lengths):
    members, tokens, _ = embeddings.shape
    blocks, cores = lax.axis_size("blk"), lax.axis_size("split")
    axes = ("blk", "split")
    far_path, side_path = z_route(blocks), x_route(blocks)
    twin_path = [(0, 1), (1, 0)]
    cuts = [HEAD + members * tokens * part // 64 // TILE * TILE for part in CUTS]
    most = cuts[-1]

    place = jnp.stack([lax.axis_index("blk") % 2, lax.axis_index("split")]).astype(jnp.float32)
    stamp = jnp.zeros((4 * members, LANES), jnp.float32).at[4 * members - 2 :].set(place[:, None])
    packed, *parts = pack(embeddings, lengths, cuts)
    fars = [lax.ppermute(part, axes, far_path) for part in parts]
    sides = [lax.ppermute(part, axes, side_path) for part in parts]
    twin = lax.ppermute(packed, "split", twin_path)

    late, over, some = score(members, 0, most, packed, twin, sides[:1], fars[:1], stamp)
    for k in range(1, len(cuts)):
        late = score(
            members, cuts[k - 1], most, packed, twin, sides[: k + 1], fars[: k + 1], late
        )[0]

    def long(late):
        rest = packed[most:]
        ahead = over > 0

        def fetch(route, colour, incoming):
            got = jnp.zeros_like(rest)
            for turn in range(2):
                pairs = [pair for pair in route if colour(pair[0] // 2, pair[0] % 2) == turn]
                sends = colour(lax.axis_index("blk"), lax.axis_index("split")) == turn
                arrived = lambda got: jnp.where(sends, got, lax.ppermute(rest, axes, pairs))
                used = jnp.where(sends, ahead[0], incoming)
                got = lax.cond(used, arrived, lambda got: got, got)
            return got

        side_rest = fetch(side_path, lambda b, s: b % 2, ahead[1])
        far_rest = fetch(far_path, lambda b, s: b // 2 % 2, ahead[2])
        return score(
            members, most, most, packed, twin, sides + [side_rest], fars + [far_rest], late
        )[0]

    scores = lax.cond(some.reshape(()) > 0, long, lambda late: late, late)
    side_scores = lax.ppermute(scores, axes, back(side_path))
    far_scores = lax.ppermute(scores, axes, back(far_path))
    twin_scores = lax.ppermute(scores, "split", twin_path)
    pair_f1, utility = assemble(scores, twin_scores, side_scores, far_scores, members)
    return (pair_f1, utility.reshape(members))


def solution(mesh):
    placed = (P(("group", "blk", "split"), None, None), P(("group", "blk", "split")))
    return jax.shard_map(
        on_device,
        mesh=mesh,
        in_specs=placed,
        out_specs=(P(("group", "blk", "split"), None, None, None), P(("group", "blk", "split"))),
        check_vma=False,
    )
```
